128 devices in a mesh: dp: 16 (over z, y_hi, core), tensor: 8 (over x, y_lo).
Axes of the slice: x: 4, y: 4 (y_hi: 2, y_lo: 2; y = y_hi * 2 + y_lo), z: 4, core: 2. Of those that a mesh axis runs over, the one named last changes fastest.
Arguments:
- encoded_neighbours: bfloat16 [128, 128, 8192], P('dp'), may hold values from -6 to 6
- kv_weight: bfloat16 [2, 8192, 4096], P(None, 'dp', 'tensor'), may hold values from -0.0625 to 0.0625
- queries: bfloat16 [4096, 4096], P('dp', 'tensor'), may hold values from -480 to 480
- out_weight: bfloat16 [4096, 8192], P('tensor'), may hold values from -0.09375 to 0.09375
- neighbour_ids: int32 [16, 4, 2, 128], P('dp'), may hold values from 0 to 31999, as said below
- slot_map: int32 [128], replicated, may hold values from 0 to 127, as said below
Outputs:
- mixed: bfloat16 [4096, 8192], P('dp', 'tensor')
The draws below stay inside these ranges and needn't reach their ends.
Inputs may be any that keep to these rules, and one draw needn't show every extreme that they name: `neighbour_ids`: 0 marks padding and only ends a neighbour; each neighbour has at least 32 tokens that are not 0, and every sequence has a neighbour without padding. `slot_map`: A permutation of the neighbours; slots i with equal i // 8 lie on one index of dp, and the 8 neighbours of one sequence lie in 8 different such blocks.
All inputs are finite; a program needn't handle non-finite values.
Results may differ from the reference program's by a relative error of at most 0.008.
The reference program's roundings to bfloat16 on the way (of `weights` and `attended`) count: a program that leaves them out, or rounds other values in their place, can miss the bound.
Values may be sent and summed in bfloat16 or wider, within the bound.
No kernel may reach another device: no remote copies, remote signals or barrier semaphores. Data moves between devices by JAX's collectives and lax.ppermute only.
A program may use at most 128 MiB of HBM per device.

```python
import math
import jax
import jax.numpy as jnp
from jax import lax

D = 8192
HEADS = 32
HD = 128
M = 64
R = 128
CPS = 4
L = 256
SEQS = 16
TOKENS = 4096
NEIGH = 128


def draw_queries(key, part):
    key = jax.random.fold_in(key, 37)
    first_key = jax.random.fold_in(key, 0)
    normal_part = jax.random.normal(first_key, (TOKENS, HEADS, HD), jnp.float32)
    values = jnp.clip(normal_part, -6.0, 6.0)
    return values.reshape(TOKENS, HEADS * HD).astype(jnp.bfloat16)


def draw_neighbour_ids(key, part):
    key = jax.random.fold_in(key, 23)
    first_key, second_key, third_key = jax.random.split(key, 3)
    device_count = NEIGH // (2 * CPS)
    tokens = jax.random.randint(first_key, (device_count, CPS, 2, R), 1, 32000)
    lengths = jax.random.randint(second_key, (device_count, CPS, 2), R // 4, R + 1)
    full_one = jax.random.randint(third_key, (device_count,), 0, 2 * CPS)
    neighbour_index = jnp.arange(2 * CPS, dtype=jnp.int32).reshape(CPS, 2)
    lengths = jnp.where(neighbour_index[None] == full_one[:, None, None], R, lengths)
    token_pos = jnp.arange(R, dtype=jnp.int32)
    return jnp.where(token_pos < lengths[..., None], tokens, 0).astype(jnp.int32)


def draw_slot_map(key, part):
    key = jax.random.fold_in(key, 11)
    first_key, second_key, third_key = jax.random.split(key, 3)
    per_seq = 2 * CPS
    device_count = NEIGH // per_seq
    offsets = jax.random.permutation(first_key, device_count)
    owner_of = jnp.argsort(offsets)
    rank_table = jax.vmap(lambda sub_key: jax.random.permutation(sub_key, per_seq))(jax.random.split(second_key, device_count))
    places = jax.vmap(lambda sub_key: jax.random.permutation(sub_key, per_seq))(jax.random.split(third_key, device_count))
    device_rows = jnp.arange(device_count, dtype=jnp.int32)[:, None]
    sequence = owner_of[(device_rows - places) % device_count]
    local_index = rank_table[sequence, places]
    return (sequence * per_seq + local_index).reshape(-1).astype(jnp.int32)


def steps_of(key, dims, shards, low, high):
    level = 1.0
    for axis_at, parts in shards:
        heights = jax.random.uniform(jax.random.fold_in(jax.random.fold_in(key, 6), axis_at), (parts,), jnp.float32, low / len(shards), high / len(shards))
        level = level * jnp.repeat(jnp.exp(heights), dims[axis_at] // parts).reshape((-1,) + (1,) * (len(dims) - 1 - axis_at))
    return level


def normal_values(own_key, dims, deviation, bound, cuts=(), kind=jnp.bfloat16):
    gain = steps_of(own_key, dims, cuts, -0.22, 0.18) if cuts else 1.0
    entries = jax.random.normal(own_key, dims, jnp.float32) * deviation * gain
    return jnp.minimum(jnp.maximum(entries, -bound), bound).astype(kind)


def setup_inputs(seed: int = 0) -> dict:
    key_list = jax.random.split(jax.random.key(seed), 7)
    encoded_neighbours = normal_values(key_list[0], (NEIGH, R, D), 1.0, 6.0, ((0, 16),))
    kv_weight = normal_values(key_list[1], (2, D, HEADS * HD), D ** -0.5, 0.0625, ((1, 16), (2, 8)))
    queries = draw_queries(jax.random.fold_in(key_list[6], 71), 0)
    out_weight = normal_values(key_list[3], (HEADS * HD, D), (HEADS * HD) ** -0.5, 0.09375, ((0, 8),))
    neighbour_ids = draw_neighbour_ids(jax.random.fold_in(key_list[6], 71), 0)
    slot_map = draw_slot_map(jax.random.fold_in(key_list[6], 71), 0)
    return {"encoded_neighbours": encoded_neighbours, "kv_weight": kv_weight, "queries": queries, "out_weight": out_weight, "neighbour_ids": neighbour_ids, "slot_map": slot_map}


def attend_stretches(query_rows, key_rows, value_rows, key_valid):
    length, columns = query_rows.shape
    stretches, key_span = key_valid.shape
    head_count = columns // HD
    lead_rows = M - 1
    shifted = jnp.concatenate([query_rows[lead_rows:], jnp.zeros((lead_rows, columns), query_rows.dtype)], axis=0)
    query_blocks = shifted.reshape(stretches, M, head_count, HD).astype(jnp.float32)
    key_blocks = key_rows.reshape(stretches, key_span, head_count, HD).astype(jnp.float32)
    value_blocks = value_rows.reshape(stretches, key_span, head_count, HD).astype(jnp.float32)
    scores = jnp.einsum('cmhd,cnhd->chmn', query_blocks, key_blocks) * (1.0 / math.sqrt(HD))
    scores = jnp.where(key_valid[:, None, None, :], scores, -jnp.inf)
    highest = lax.optimization_barrier(jnp.max(scores, axis=-1, keepdims=True))
    raised = jnp.exp(scores - highest)
    weights = (raised / lax.optimization_barrier(jnp.sum(raised, axis=-1, keepdims=True))).astype(jnp.bfloat16)
    mixed_heads = jnp.einsum('chmn,cnhd->cmhd', weights.astype(jnp.float32), value_blocks).astype(jnp.bfloat16)
    flat_rows = mixed_heads.reshape(stretches * M, columns)
    return jnp.concatenate([jnp.zeros((lead_rows, columns), jnp.bfloat16), flat_rows[:length - lead_rows]], axis=0)

def reference(encoded_neighbours, kv_weight, queries, out_weight, neighbour_ids, slot_map):
    columns = HEADS * HD
    stacked = encoded_neighbours.reshape(NEIGH * R, D)
    key_slots = jnp.dot(stacked, kv_weight[0], preferred_element_type=jnp.float32).astype(jnp.bfloat16)
    value_slots = jnp.dot(stacked, kv_weight[1], preferred_element_type=jnp.float32).astype(jnp.bfloat16)
    slot_of = jnp.zeros((NEIGH,), jnp.int32).at[slot_map].set(jnp.arange(NEIGH, dtype=jnp.int32))
    stretch_keys = key_slots.reshape(NEIGH, R, columns)[slot_of].reshape(SEQS, CPS, 2 * R, columns)
    stretch_values = value_slots.reshape(NEIGH, R, columns)[slot_of].reshape(SEQS, CPS, 2 * R, columns)
    key_valid = neighbour_ids.reshape(SEQS, CPS, 2 * R) != 0
    query_rows = queries.reshape(SEQS, L, columns)
    attended = lax.map(lambda members: attend_stretches(*members), (query_rows, stretch_keys, stretch_values, key_valid))
    return jnp.dot(attended.reshape(TOKENS, columns), out_weight, preferred_element_type=jnp.float32).astype(jnp.bfloat16)
```

```python
import functools
import math

import jax
import jax.numpy as jnp
from jax import lax
from jax.experimental import pallas as pl
from jax.experimental.pallas import tpu as pltpu
from jax.sharding import PartitionSpec as P

HD = 128
M = 64
BF = jnp.bfloat16
F32 = jnp.float32
VMEM_LIMIT = 48 * 1024 * 1024


def dp_pairs(dz, dy, dc):
    pairs = []
    for i in range(16):
        z, y, c = i // 4, (i // 2) % 2, i % 2
        pairs.append((i, ((z + dz) % 4) * 4 + ((y + dy) % 2) * 2 + (c + dc) % 2))
    return pairs


def tensor_pairs(dx, dy):
    pairs = []
    for i in range(8):
        x, y = i // 2, i % 2
        pairs.append((i, ((x + dx) % 4) * 2 + (y + dy) % 2))
    return pairs


Z_UP, Z_DOWN = dp_pairs(1, 0, 0), dp_pairs(-1, 0, 0)
Y_SWAP, CORE_SWAP = dp_pairs(0, 1, 0), dp_pairs(0, 0, 1)


def vmem_specs(count):
    return [pl.BlockSpec(memory_space=pltpu.VMEM)] * count


def project_kernel(blocks, has_total, final, idx, *refs):
    del idx
    rows = refs[:blocks]
    weights = refs[blocks : 2 * blocks]
    rest = refs[2 * blocks :]
    out = rest[-1]
    columns = weights[0].shape[2]
    for side in range(2):
        cols = slice(side * columns, (side + 1) * columns)
        total = rest[0][:, cols] if has_total else None
        for row, weight in zip(rows, weights):
            term = jnp.dot(row[...], weight[side], preferred_element_type=F32)
            total = term if total is None else total + term
        out[:, cols] = total.astype(out.dtype)


def project(encoded, pieces, total, final):
    rows = encoded.shape[0]
    depth, columns = pieces[0][1].shape[1:]
    tile = 256
    blocks = len(pieces)
    idx = jnp.stack([place for place, _ in pieces]).astype(jnp.int32)

    def row_spec(j):
        return pl.BlockSpec((tile, depth), lambda m, i, j=j: (m, i[j]))

    in_specs = [row_spec(j) for j in range(blocks)] + [
        pl.BlockSpec((2, depth, columns), lambda m, i: (0, 0, 0), pipeline_mode=pl.Buffered(1))
    ] * blocks
    operands = [encoded] * blocks + [weight for _, weight in pieces]
    total_spec = pl.BlockSpec((tile, 2 * columns), lambda m, i: (m, 0))
    if total is not None:
        in_specs.append(total_spec)
        operands.append(total)
    return pl.pallas_call(
        functools.partial(project_kernel, blocks, total is not None, final),
        grid_spec=pltpu.PrefetchScalarGridSpec(
            num_scalar_prefetch=1, grid=(rows // tile,), in_specs=in_specs, out_specs=total_spec
        ),
        out_shape=jax.ShapeDtypeStruct((rows, 2 * columns), BF if final else F32),
        compiler_params=pltpu.CompilerParams(vmem_limit_bytes=VMEM_LIMIT),
        cost_estimate=pl.CostEstimate(
            flops=4 * rows * depth * columns * blocks,
            bytes_accessed=2 * blocks * depth * (rows + 2 * columns),
            transcendentals=0,
        ),
        name="project",
    )(idx, *operands)


def pack_kernel(holder, query, valid, out):
    rows = query.shape[0]
    shifted = pltpu.roll(query[...].astype(F32), rows - (M - 1), 0).astype(BF)
    for j in range(valid.shape[0]):
        u = j // 2
        out[holder[j], :M, :] = shifted[u * M : (u + 1) * M]
        out[holder[j], M:, :] = jnp.tile(valid[j : j + 1, :], (16, query.shape[1] // HD)).astype(BF)


def pack_queries(query, valid, holder, groups):
    return pl.pallas_call(
        pack_kernel,
        in_specs=[pl.BlockSpec(memory_space=pltpu.SMEM)] + vmem_specs(2),
        out_specs=pl.BlockSpec(memory_space=pltpu.VMEM),
        out_shape=jax.ShapeDtypeStruct((groups, M + 16, query.shape[1]), BF),
        compiler_params=pltpu.CompilerParams(vmem_limit_bytes=VMEM_LIMIT),
        name="pack_queries",
    )(holder, query, valid)


def attend_kernel(owner, query, keys_values, out):
    del owner
    heads = query.shape[2] // HD
    span = keys_values.shape[0]
    valid = query[0, M : M + 1, :span].astype(F32) > 0.5
    lane = lax.broadcasted_iota(jnp.int32, (M, HD), 1)
    stats = jnp.zeros((M, HD), F32)
    for h in range(heads):
        cols = slice(h * HD, (h + 1) * HD)
        value_cols = slice((heads + h) * HD, (heads + h + 1) * HD)
        scores = lax.dot_general(
            query[0, :M, cols],
            keys_values[:, cols],
            (((1,), (1,)), ((), ())),
            preferred_element_type=F32,
        ) * (1.0 / math.sqrt(HD))
        scores = jnp.where(valid, scores, -jnp.inf)
        highest = jnp.max(scores, axis=1, keepdims=True)
        raised = jnp.exp(scores - highest)
        norm = jnp.sum(raised, axis=1, keepdims=True)
        weights = (raised / norm).astype(BF)
        out[0, :, cols] = jnp.dot(
            weights, keys_values[:, value_cols], preferred_element_type=F32
        ).astype(BF)
        level = highest + jnp.log(norm)
        first = level.astype(BF).astype(F32)
        second = (level - first).astype(BF).astype(F32)
        third = level - first - second
        stats = jnp.where(lane == 3 * h, first, stats)
        stats = jnp.where(lane == 3 * h + 1, second, stats)
        stats = jnp.where(lane == 3 * h + 2, third, stats)
    out[0, :, heads * HD :] = stats.astype(BF)


def attend(owner, query_blocks, keys_values, span):
    groups, query_rows, columns = query_blocks.shape
    slots = keys_values.shape[0] // span
    return pl.pallas_call(
        attend_kernel,
        grid_spec=pltpu.PrefetchScalarGridSpec(
            num_scalar_prefetch=1,
            grid=(slots,),
            in_specs=[
                pl.BlockSpec((1, query_rows, columns), lambda i, owner: (owner[i], 0, 0)),
                pl.BlockSpec((span, 2 * columns), lambda i, owner: (i, 0)),
            ],
            out_specs=pl.BlockSpec((1, M, columns + HD), lambda i, owner: (owner[i], 0, 0)),
        ),
        out_shape=jax.ShapeDtypeStruct((groups, M, columns + HD), BF),
        compiler_params=pltpu.CompilerParams(vmem_limit_bytes=VMEM_LIMIT),
        name="attend",
    )(owner, query_blocks, keys_values)


def combine_kernel(holder, parts, out):
    rows, columns = out.shape
    heads = columns // HD
    flat = []
    for u in range(rows // M):
        first, second = parts[holder[2 * u]], parts[holder[2 * u + 1]]
        levels = [part[:, columns:].astype(F32) for part in (first, second)]
        pieces = []
        for h in range(heads):
            cols = slice(h * HD, (h + 1) * HD)
            one, two = [
                level[:, 3 * h : 3 * h + 1]
                + level[:, 3 * h + 1 : 3 * h + 2]
                + level[:, 3 * h + 2 : 3 * h + 3]
                for level in levels
            ]
            top = jnp.maximum(one, two)
            share_one, share_two = jnp.exp(one - top), jnp.exp(two - top)
            both = share_one + share_two
            pieces.append(
                first[:, cols].astype(F32) * (share_one / both)
                + second[:, cols].astype(F32) * (share_two / both)
            )
        flat.append(jnp.concatenate(pieces, axis=1))
    shifted = pltpu.roll(jnp.concatenate(flat, axis=0), M - 1, 0)
    row = lax.broadcasted_iota(jnp.int32, (rows, columns), 0)
    out[...] = jnp.where(row >= M - 1, shifted, 0.0).astype(BF)


def combine(holder, parts, rows):
    columns = parts.shape[2] - HD
    return pl.pallas_call(
        combine_kernel,
        in_specs=[pl.BlockSpec(memory_space=pltpu.SMEM)] + vmem_specs(1),
        out_specs=pl.BlockSpec(memory_space=pltpu.VMEM),
        out_shape=jax.ShapeDtypeStruct((rows, columns), BF),
        compiler_params=pltpu.CompilerParams(vmem_limit_bytes=VMEM_LIMIT),
        name="combine",
    )(holder, parts)


def mix_kernel(place, *refs):
    attended = refs[:4]
    mine, other, out = refs[4:]
    core = place[5]
    half = mine.shape[1]
    total = None
    for r in range(4):
        for swap, weight in ((0, mine), (1, other)):
            cols = pl.ds(pl.multiple_of(((core + swap) % 2) * half, half), half)
            term = jnp.dot(attended[r][:, cols], weight[place[r]], preferred_element_type=F32)
            total = term if total is None else total + term
    out[...] = total.astype(out.dtype)


def mix(place, attended, mine, other, kind):
    rows, columns = attended[0].shape
    width = mine.shape[2] // 2
    tile = width // 2
    weight_spec = pl.BlockSpec(
        (4, mine.shape[1], tile), lambda j, place: (0, 0, place[4] * 2 + j)
    )
    return pl.pallas_call(
        mix_kernel,
        grid_spec=pltpu.PrefetchScalarGridSpec(
            num_scalar_prefetch=1,
            grid=(2,),
            in_specs=[pl.BlockSpec((rows, columns), lambda j, place: (0, 0))] * 4
            + [weight_spec] * 2,
            out_specs=pl.BlockSpec((rows, tile), lambda j, place: (0, j)),
        ),
        out_shape=jax.ShapeDtypeStruct((rows, width), kind),
        compiler_params=pltpu.CompilerParams(vmem_limit_bytes=VMEM_LIMIT),
        cost_estimate=pl.CostEstimate(
            flops=8 * rows * columns * width, bytes_accessed=8 * columns * width, transcendentals=0
        ),
        name="mix",
    )(place, *attended, mine, other)


def gather_weights(own, position):
    z, y, c = position // 4, (position // 2) % 2, position % 2

    def at(dz, dy, dc):
        return ((z + dz) % 4) * 4 + ((y + dy) % 2) * 2 + (c + dc) % 2

    def send(block, pairs):
        return lax.ppermute(block, "dp", pairs)

    def with_twin(block, dz, dy):
        return [(at(dz, dy, 0), block), (at(dz, dy, 1), send(block, CORE_SWAP))]

    below, above, across = send(own, Z_UP), send(own, Z_DOWN), send(own, Y_SWAP)
    far = send(above, Z_DOWN)
    across_below = send(across, Z_UP)
    across_above = send(above, Y_SWAP)
    across_far = jnp.concatenate(
        [send(across_below[:1], Z_UP), send(across_above[1:], Z_DOWN)], axis=0
    )
    return [
        with_twin(own, 0, 0)
        + with_twin(below, -1, 0)
        + with_twin(above, 1, 0)
        + with_twin(across, 0, 1),
        with_twin(far, 2, 0) + with_twin(across_below, -1, 1) + with_twin(across_above, 1, 1),
        with_twin(across_far, 2, 1),
    ]


def body(encoded_neighbours, kv_weight, queries, out_weight, neighbour_ids, slot_map):
    groups = lax.axis_size("dp")
    position = lax.axis_index("dp")
    tensor_at = lax.axis_index("tensor")
    core, x, y_lo = position % 2, tensor_at // 2, tensor_at % 2
    slot_count, span, model_width = encoded_neighbours.shape
    encoded = encoded_neighbours.reshape(slot_count * span, model_width)

    held = lax.dynamic_slice_in_dim(slot_map, position * slot_count, slot_count)
    owner = held // slot_count
    wanted = position * slot_count + jnp.arange(slot_count, dtype=jnp.int32)
    holder = (
        jnp.sum(
            jnp.where(
                slot_map[None, :] == wanted[:, None],
                jnp.arange(slot_map.shape[0], dtype=jnp.int32)[None, :],
                0,
            ),
            axis=1,
        )
        // slot_count
    )
    valid = (neighbour_ids.reshape(slot_count, span) != 0).astype(F32)
    outgoing = pack_queries(queries, valid, holder, groups)
    query_blocks = lax.all_to_all(outgoing, "dp", 0, 0, tiled=True)

    half = out_weight.shape[0] // 2
    x_size = 4
    pair_width = out_weight.shape[1] // x_size
    own_half = lax.dynamic_slice_in_dim(out_weight, core * half, half, 0)
    own_half = own_half.reshape(half, x_size, pair_width).transpose(1, 0, 2)
    x_groups = [[i * 2 + yl for i in range(x_size)] for yl in range(2)]
    mix_mine = lax.all_to_all(own_half, "tensor", 0, 0, tiled=True, axis_index_groups=x_groups)
    mix_other = lax.ppermute(mix_mine, "dp", CORE_SWAP)

    stages = gather_weights(kv_weight, position)
    total = None
    for at, stage in enumerate(stages):
        total = project(encoded, stage, total, at == len(stages) - 1)

    parts = attend(owner, query_blocks, total, span)
    returned = lax.all_to_all(parts, "dp", 0, 0, tiled=True)
    attended = combine(holder, returned, queries.shape[0])

    near = [
        attended,
        lax.ppermute(attended, "tensor", tensor_pairs(1, 0)),
        lax.ppermute(attended, "tensor", tensor_pairs(-1, 0)),
        lax.ppermute(attended, "tensor", tensor_pairs(2, 0)),
    ]
    places = [x, (x + 3) % 4, (x + 1) % 4, (x + 2) % 4]
    theirs = mix(jnp.stack(places + [1 - y_lo, core]), near, mix_mine, mix_other, BF)
    arrived = lax.ppermute(theirs, "tensor", tensor_pairs(0, 1))
    ours = mix(jnp.stack(places + [y_lo, core]), near, mix_mine, mix_other, F32)
    return (ours + arrived.astype(F32)).astype(BF)


def solution(mesh):
    placed = (
        P("dp", None, None),
        P(None, "dp", "tensor"),
        P("dp", "tensor"),
        P("tensor", None),
        P("dp", None, None, None),
        P(),
    )
    return jax.shard_map(
        body, mesh=mesh, in_specs=placed, out_specs=P("dp", "tensor"), check_vma=False
    )
```

```python
import functools
import math

import jax
import jax.numpy as jnp
from jax import lax
from jax.experimental import pallas as pl
from jax.experimental.pallas import tpu as pltpu
from jax.sharding import PartitionSpec as P

HD = 128
M = 64
BF = jnp.bfloat16
F32 = jnp.float32
ATTEND_SLOTS = 2
VMEM_LIMIT = 48 * 1024 * 1024


def dp_pairs(dz, dy, dc):
    pairs = []
    for i in range(16):
        z, y, c = i // 4, (i // 2) % 2, i % 2
        pairs.append((i, ((z + dz) % 4) * 4 + ((y + dy) % 2) * 2 + (c + dc) % 2))
    return pairs


def tensor_pairs(dx, dy):
    pairs = []
    for i in range(8):
        x, y = i // 2, i % 2
        pairs.append((i, ((x + dx) % 4) * 2 + (y + dy) % 2))
    return pairs


Z_UP, Z_DOWN = dp_pairs(1, 0, 0), dp_pairs(-1, 0, 0)
Y_SWAP, CORE_SWAP = dp_pairs(0, 1, 0), dp_pairs(0, 0, 1)


def vmem_specs(count):
    return [pl.BlockSpec(memory_space=pltpu.VMEM)] * count


def project_kernel(sizes, has_total, idx, *refs):
    del idx
    blocks = len(sizes)
    rows = refs[:blocks]
    weights = []
    at = blocks
    for size in sizes:
        if size == 1:
            weights.append((refs[at].at[0], refs[at].at[1]))
        else:
            weights.append((refs[at].at[0], refs[at + 1].at[0]))
        at += size
    out = refs[-1]
    columns = out.shape[1] // 2
    for side in range(2):
        cols = slice(side * columns, (side + 1) * columns)
        total = refs[at][:, cols] if has_total else None
        for row, weight in zip(rows, weights):
            term = jnp.dot(row[...], weight[side][...], preferred_element_type=F32)
            total = term if total is None else total + term
        out[:, cols] = total.astype(out.dtype)


def project(encoded, pieces, total, final):
    rows = encoded.shape[0]
    arrays = [array for _, weight in pieces for array in weight]
    depth, columns = arrays[0].shape[1:]
    tile = 256
    blocks = len(pieces)
    idx = jnp.stack([place for place, _ in pieces]).astype(jnp.int32)

    def row_spec(j):
        return pl.BlockSpec((tile, depth), lambda m, i, j=j: (m, i[j]))

    in_specs = [row_spec(j) for j in range(blocks)] + [
        pl.BlockSpec(array.shape, lambda m, i: (0, 0, 0), pipeline_mode=pl.Buffered(1))
        for array in arrays
    ]
    operands = [encoded] * blocks + arrays
    total_spec = pl.BlockSpec((tile, 2 * columns), lambda m, i: (m, 0))
    if total is not None:
        in_specs.append(total_spec)
        operands.append(total)
    return pl.pallas_call(
        functools.partial(project_kernel, [len(w) for _, w in pieces], total is not None),
        grid_spec=pltpu.PrefetchScalarGridSpec(
            num_scalar_prefetch=1, grid=(rows // tile,), in_specs=in_specs, out_specs=total_spec
        ),
        out_shape=jax.ShapeDtypeStruct((rows, 2 * columns), BF if final else F32),
        compiler_params=pltpu.CompilerParams(vmem_limit_bytes=VMEM_LIMIT),
        cost_estimate=pl.CostEstimate(
            flops=4 * rows * depth * columns * blocks,
            bytes_accessed=2 * blocks * depth * (rows + 2 * columns),
            transcendentals=0,
        ),
        name="project",
    )(idx, *operands)


def split_kernel(core, rows, out):
    del core
    out[0] = rows[...]


def split_rows(core, weight, parts):
    half, width = weight.shape[0] // 2, weight.shape[1] // parts
    return pl.pallas_call(
        split_kernel,
        grid_spec=pltpu.PrefetchScalarGridSpec(
            num_scalar_prefetch=1,
            grid=(parts,),
            in_specs=[pl.BlockSpec((half, width), lambda j, core: (core[0], j))],
            out_specs=pl.BlockSpec((1, half, width), lambda j, core: (j, 0, 0)),
        ),
        out_shape=jax.ShapeDtypeStruct((parts, half, width), weight.dtype),
        compiler_params=pltpu.CompilerParams(vmem_limit_bytes=VMEM_LIMIT),
        cost_estimate=pl.CostEstimate(
            flops=0, bytes_accessed=8 * half * width * parts, transcendentals=0
        ),
        name="split_rows",
    )(core, weight)


def pack_kernel(holder, query, valid, out):
    rows = query.shape[0]
    shifted = pltpu.roll(query[...].astype(F32), rows - (M - 1), 0).astype(BF)
    for j in range(valid.shape[0]):
        u = j // 2
        out[holder[j], :M, :] = shifted[u * M : (u + 1) * M]
        out[holder[j], M:, :] = jnp.tile(valid[j : j + 1, :], (16, query.shape[1] // HD)).astype(BF)


def pack_queries(query, valid, holder, groups):
    return pl.pallas_call(
        pack_kernel,
        in_specs=[pl.BlockSpec(memory_space=pltpu.SMEM)] + vmem_specs(2),
        out_specs=pl.BlockSpec(memory_space=pltpu.VMEM),
        out_shape=jax.ShapeDtypeStruct((groups, M + 16, query.shape[1]), BF),
        compiler_params=pltpu.CompilerParams(vmem_limit_bytes=VMEM_LIMIT),
        name="pack_queries",
    )(holder, query, valid)


def attend_kernel(owner, query, keys_values, out):
    heads = query.shape[2] // HD
    span = keys_values.shape[0] // ATTEND_SLOTS
    lane = lax.broadcasted_iota(jnp.int32, (M, HD), 1)
    pairs = [(i, h) for i in range(ATTEND_SLOTS) for h in range(heads)]
    places = [owner[pl.program_id(0) * ATTEND_SLOTS + i] for i in range(ATTEND_SLOTS)]
    scores = {}
    for i, h in pairs:
        cols = slice(h * HD, (h + 1) * HD)
        scores[i, h] = lax.dot_general(
            query[places[i], :M, cols],
            keys_values[i * span : (i + 1) * span, cols],
            (((1,), (1,)), ((), ())),
            preferred_element_type=F32,
        )
    valid = [query[place, M : M + 1, :span].astype(F32) > 0.5 for place in places]
    weights, levels = {}, {}
    for i, h in pairs:
        scaled = jnp.where(valid[i], scores[i, h] * (1.0 / math.sqrt(HD)), -jnp.inf)
        highest = jnp.max(scaled, axis=1, keepdims=True)
        raised = jnp.exp(scaled - highest)
        norm = jnp.sum(raised, axis=1, keepdims=True)
        weights[i, h] = (raised / norm).astype(BF)
        levels[i, h] = highest + jnp.log(norm)
    for i, h in pairs:
        out[places[i], :, h * HD : (h + 1) * HD] = jnp.dot(
            weights[i, h],
            keys_values[i * span : (i + 1) * span, (heads + h) * HD : (heads + h + 1) * HD],
            preferred_element_type=F32,
        ).astype(BF)
    for i in range(ATTEND_SLOTS):
        stats = jnp.zeros((M, HD), F32)
        for h in range(heads):
            first = levels[i, h].astype(BF).astype(F32)
            second = (levels[i, h] - first).astype(BF).astype(F32)
            third = levels[i, h] - first - second
            stats = jnp.where(lane == 3 * h, first, stats)
            stats = jnp.where(lane == 3 * h + 1, second, stats)
            stats = jnp.where(lane == 3 * h + 2, third, stats)
        out[places[i], :, heads * HD :] = stats.astype(BF)


def attend(owner, query_blocks, keys_values, span):
    groups, query_rows, columns = query_blocks.shape
    steps = keys_values.shape[0] // (span * ATTEND_SLOTS)
    return pl.pallas_call(
        attend_kernel,
        grid_spec=pltpu.PrefetchScalarGridSpec(
            num_scalar_prefetch=1,
            grid=(steps,),
            in_specs=[
                pl.BlockSpec((groups, query_rows, columns), lambda i, owner: (0, 0, 0)),
                pl.BlockSpec((span * ATTEND_SLOTS, 2 * columns), lambda i, owner: (i, 0)),
            ],
            out_specs=pl.BlockSpec((groups, M, columns + HD), lambda i, owner: (0, 0, 0)),
        ),
        out_shape=jax.ShapeDtypeStruct((groups, M, columns + HD), BF),
        compiler_params=pltpu.CompilerParams(vmem_limit_bytes=VMEM_LIMIT),
        name="attend",
    )(owner, query_blocks, keys_values)


def combine_kernel(holder, parts, out):
    rows, columns = out.shape
    heads = columns // HD
    flat = []
    for u in range(rows // M):
        first, second = parts[holder[2 * u]], parts[holder[2 * u + 1]]
        levels = [part[:, columns:].astype(F32) for part in (first, second)]
        pieces = []
        for h in range(heads):
            cols = slice(h * HD, (h + 1) * HD)
            one, two = [
                level[:, 3 * h : 3 * h + 1]
                + level[:, 3 * h + 1 : 3 * h + 2]
                + level[:, 3 * h + 2 : 3 * h + 3]
                for level in levels
            ]
            top = jnp.maximum(one, two)
            share_one, share_two = jnp.exp(one - top), jnp.exp(two - top)
            both = share_one + share_two
            pieces.append(
                first[:, cols].astype(F32) * (share_one / both)
                + second[:, cols].astype(F32) * (share_two / both)
            )
        flat.append(jnp.concatenate(pieces, axis=1))
    shifted = pltpu.roll(jnp.concatenate(flat, axis=0), M - 1, 0)
    row = lax.broadcasted_iota(jnp.int32, (rows, columns), 0)
    out[...] = jnp.where(row >= M - 1, shifted, 0.0).astype(BF)


def combine(holder, parts, rows):
    columns = parts.shape[2] - HD
    return pl.pallas_call(
        combine_kernel,
        in_specs=[pl.BlockSpec(memory_space=pltpu.SMEM)] + vmem_specs(1),
        out_specs=pl.BlockSpec(memory_space=pltpu.VMEM),
        out_shape=jax.ShapeDtypeStruct((rows, columns), BF),
        compiler_params=pltpu.CompilerParams(vmem_limit_bytes=VMEM_LIMIT),
        name="combine",
    )(holder, parts)


def mix_kernel(place, *refs):
    attended = refs[:4]
    mine, other, out = refs[4:]
    core = place[5]
    half = mine.shape[1]
    total = None
    for r in range(4):
        for swap, weight in ((0, mine), (1, other)):
            cols = pl.ds(pl.multiple_of(((core + swap) % 2) * half, half), half)
            term = jnp.dot(attended[r][:, cols], weight[place[r]], preferred_element_type=F32)
            total = term if total is None else total + term
    out[...] = total.astype(out.dtype)


def mix(place, attended, mine, other, kind):
    rows, columns = attended[0].shape
    width = mine.shape[2] // 2
    tile = width // 2
    weight_spec = pl.BlockSpec(
        (4, mine.shape[1], tile), lambda j, place: (0, 0, place[4] * 2 + j)
    )
    return pl.pallas_call(
        mix_kernel,
        grid_spec=pltpu.PrefetchScalarGridSpec(
            num_scalar_prefetch=1,
            grid=(2,),
            in_specs=[pl.BlockSpec((rows, columns), lambda j, place: (0, 0))] * 4
            + [weight_spec] * 2,
            out_specs=pl.BlockSpec((rows, tile), lambda j, place: (0, j)),
        ),
        out_shape=jax.ShapeDtypeStruct((rows, width), kind),
        compiler_params=pltpu.CompilerParams(vmem_limit_bytes=VMEM_LIMIT),
        cost_estimate=pl.CostEstimate(
            flops=8 * rows * columns * width, bytes_accessed=8 * columns * width, transcendentals=0
        ),
        name="mix",
    )(place, *attended, mine, other)


def project_gathered(encoded, own, own_twin, position, query_blocks, core):
    z, y, c = position // 4, (position // 2) % 2, position % 2

    def send(block, pairs):
        return lax.ppermute(block, "dp", pairs)

    def with_twin(dz, dy, *arrays):
        def at(dc):
            return ((z + dz) % 4) * 4 + ((y + dy) % 2) * 2 + (c + dc) % 2

        return [(at(0), arrays), (at(1), tuple(send(array, CORE_SWAP) for array in arrays))]

    below, above, across = send(own, Z_UP), send(own, Z_DOWN), send(own, Y_SWAP)
    own_pieces = [(position, (own,)), (position + 1 - 2 * c, (own_twin,))]
    below, above, across, query_blocks, core = lax.optimization_barrier(
        (below, above, across, query_blocks, core)
    )
    far, across_below, across_above = send(above, Z_DOWN), send(across, Z_UP), send(above, Y_SWAP)
    total = project(
        encoded,
        own_pieces
        + with_twin(-1, 0, below)
        + with_twin(1, 0, above)
        + with_twin(0, 1, across),
        None,
        False,
    )
    far, across_below, across_above, total = lax.optimization_barrier(
        (far, across_below, across_above, total)
    )
    far_keys, far_values = send(across_below[:1], Z_UP), send(across_above[1:], Z_DOWN)
    total = project(
        encoded,
        with_twin(2, 0, far) + with_twin(-1, 1, across_below) + with_twin(1, 1, across_above),
        total,
        False,
    )
    far_keys, far_values, total = lax.optimization_barrier((far_keys, far_values, total))
    last = project(encoded, with_twin(2, 1, far_keys, far_values), total, True)
    return last, query_blocks, core


def body(encoded_neighbours, kv_weight, queries, out_weight, neighbour_ids, slot_map):
    groups = lax.axis_size("dp")
    position = lax.axis_index("dp")
    tensor_at = lax.axis_index("tensor")
    core, x, y_lo = position % 2, tensor_at // 2, tensor_at % 2
    slot_count, span, model_width = encoded_neighbours.shape
    encoded = encoded_neighbours.reshape(slot_count * span, model_width)

    held = lax.dynamic_slice_in_dim(slot_map, position * slot_count, slot_count)
    owner = held // slot_count
    wanted = position * slot_count + jnp.arange(slot_count, dtype=jnp.int32)
    holder = (
        jnp.sum(
            jnp.where(
                slot_map[None, :] == wanted[:, None],
                jnp.arange(slot_map.shape[0], dtype=jnp.int32)[None, :],
                0,
            ),
            axis=1,
        )
        // slot_count
    )
    valid = (neighbour_ids.reshape(slot_count, span) != 0).astype(F32)
    own_twin = lax.ppermute(kv_weight, "dp", CORE_SWAP)
    own_twin, holder = lax.optimization_barrier((own_twin, holder))
    outgoing = pack_queries(queries, valid, holder, groups)
    query_blocks = lax.all_to_all(outgoing, "dp", 0, 0, tiled=True)

    keys_values, query_blocks, later_core = project_gathered(
        encoded, kv_weight, own_twin, position, query_blocks, jnp.full((1,), core, jnp.int32)
    )

    x_size = 4
    own_half = split_rows(later_core, out_weight, x_size)
    x_groups = [[i * 2 + yl for i in range(x_size)] for yl in range(2)]
    mix_mine = lax.all_to_all(own_half, "tensor", 0, 0, tiled=True, axis_index_groups=x_groups)
    mix_mine, keys_values = lax.optimization_barrier((mix_mine, keys_values))
    mix_other = lax.ppermute(mix_mine, "dp", CORE_SWAP)

    parts = attend(owner, query_blocks, keys_values, span)
    returned = lax.all_to_all(parts, "dp", 0, 0, tiled=True)
    attended = combine(holder, returned, queries.shape[0])

    near = [
        attended,
        lax.ppermute(attended, "tensor", tensor_pairs(1, 0)),
        lax.ppermute(attended, "tensor", tensor_pairs(-1, 0)),
        lax.ppermute(attended, "tensor", tensor_pairs(2, 0)),
    ]
    places = [x, (x + 3) % 4, (x + 1) % 4, (x + 2) % 4]
    theirs = mix(jnp.stack(places + [1 - y_lo, core]), near, mix_mine, mix_other, BF)
    arrived = lax.ppermute(theirs, "tensor", tensor_pairs(0, 1))
    ours = mix(jnp.stack(places + [y_lo, core]), near, mix_mine, mix_other, F32)
    return (ours + arrived.astype(F32)).astype(BF)


def solution(mesh):
    placed = (
        P("dp", None, None),
        P(None, "dp", "tensor"),
        P("dp", "tensor"),
        P("tensor", None),
        P("dp", None, None, None),
        P(),
    )
    return jax.shard_map(
        body, mesh=mesh, in_specs=placed, out_specs=P("dp", "tensor"), check_vma=False
    )
```

```python
import functools
import math

import jax
import jax.numpy as jnp
from jax import lax
from jax.experimental import pallas as pl
from jax.experimental.pallas import tpu as pltpu
from jax.sharding import PartitionSpec as P

HD = 128
M = 64
BF = jnp.bfloat16
F32 = jnp.float32
ATTEND_SLOTS = 2
VMEM_LIMIT = 48 * 1024 * 1024


def dp_pairs(dz, dy, dc):
    pairs = []
    for i in range(16):
        z, y, c = i // 4, (i // 2) % 2, i % 2
        pairs.append((i, ((z + dz) % 4) * 4 + ((y + dy) % 2) * 2 + (c + dc) % 2))
    return pairs


def tensor_pairs(dx, dy):
    pairs = []
    for i in range(8):
        x, y = i // 2, i % 2
        pairs.append((i, ((x + dx) % 4) * 2 + (y + dy) % 2))
    return pairs


Z_UP, Z_DOWN = dp_pairs(1, 0, 0), dp_pairs(-1, 0, 0)
Y_SWAP, CORE_SWAP = dp_pairs(0, 1, 0), dp_pairs(0, 0, 1)


def vmem_specs(count):
    return [pl.BlockSpec(memory_space=pltpu.VMEM)] * count


def add_terms(sizes, rows, weight_refs, total, out):
    weights = []
    at = 0
    for size in sizes:
        if size == 1:
            weights.append((weight_refs[at].at[0], weight_refs[at].at[1]))
        else:
            weights.append((weight_refs[at].at[0], weight_refs[at + 1].at[0]))
        at += size
    columns = out.shape[1] // 2
    for side in range(2):
        cols = slice(side * columns, (side + 1) * columns)
        value = None if total is None else total[:, cols]
        for row, weight in zip(rows, weights):
            term = jnp.dot(row[...], weight[side][...], preferred_element_type=F32)
            value = term if value is None else value + term
        out[:, cols] = value.astype(out.dtype)


def project_kernel(sizes, has_total, idx, *refs):
    del idx
    blocks = len(sizes)
    rows, weights = refs[:blocks], refs[blocks : blocks + sum(sizes)]
    add_terms(sizes, rows, weights, refs[-2] if has_total else None, refs[-1])


def project_operands(encoded, pieces, tile):
    arrays = [array for _, weight in pieces for array in weight]
    depth = arrays[0].shape[1]
    specs = [
        pl.BlockSpec((tile, depth), lambda m, i, j=j: (m, i[j])) for j in range(len(pieces))
    ] + [
        pl.BlockSpec(array.shape, lambda m, i: (0, 0, 0), pipeline_mode=pl.Buffered(1))
        for array in arrays
    ]
    return specs, [encoded] * len(pieces) + arrays


def project(encoded, pieces, total):
    rows = encoded.shape[0]
    depth, columns = pieces[0][1][0].shape[1:]
    tile = 256
    in_specs, operands = project_operands(encoded, pieces, tile)
    total_spec = pl.BlockSpec((tile, 2 * columns), lambda m, i: (m, 0))
    if total is not None:
        in_specs.append(total_spec)
        operands.append(total)
    return pl.pallas_call(
        functools.partial(project_kernel, [len(w) for _, w in pieces], total is not None),
        grid_spec=pltpu.PrefetchScalarGridSpec(
            num_scalar_prefetch=1, grid=(rows // tile,), in_specs=in_specs, out_specs=total_spec
        ),
        out_shape=jax.ShapeDtypeStruct((rows, 2 * columns), F32),
        compiler_params=pltpu.CompilerParams(vmem_limit_bytes=VMEM_LIMIT),
        cost_estimate=pl.CostEstimate(
            flops=4 * rows * depth * columns * len(pieces),
            bytes_accessed=2 * len(pieces) * depth * (rows + 2 * columns),
            transcendentals=0,
        ),
        name="project",
    )(jnp.stack([place for place, _ in pieces]).astype(jnp.int32), *operands)


def split_kernel(place, *refs):
    del place
    count = len(refs) // 2
    for source, target in zip(refs[:count], refs[count:]):
        target[...] = source[...]


def split_rows(core, places, weight):
    parts = len(places)
    half, width = weight.shape[0] // 2, weight.shape[1] // parts
    tile = half // 4
    return pl.pallas_call(
        split_kernel,
        grid_spec=pltpu.PrefetchScalarGridSpec(
            num_scalar_prefetch=1,
            grid=(4,),
            in_specs=[
                pl.BlockSpec((tile, width), lambda m, place, r=r: (place[parts] * 4 + m, place[r]))
                for r in range(parts)
            ],
            out_specs=[pl.BlockSpec((tile, width), lambda m, place: (m, 0))] * parts,
        ),
        out_shape=[jax.ShapeDtypeStruct((half, width), weight.dtype)] * parts,
        compiler_params=pltpu.CompilerParams(vmem_limit_bytes=VMEM_LIMIT),
        cost_estimate=pl.CostEstimate(
            flops=0, bytes_accessed=half * width // 8, transcendentals=0
        ),
        name="split_rows",
    )(jnp.stack(places + [core]), *[weight] * parts)


def pack_kernel(holder, query, valid, out):
    rows = query.shape[0]
    shifted = pltpu.roll(query[...].astype(F32), rows - (M - 1), 0).astype(BF)
    for j in range(valid.shape[0]):
        u = j // 2
        out[holder[j], :M, :] = shifted[u * M : (u + 1) * M]
        out[holder[j], M:, :] = jnp.tile(valid[j : j + 1, :], (16, query.shape[1] // HD)).astype(BF)


def pack_queries(query, valid, holder, groups):
    return pl.pallas_call(
        pack_kernel,
        in_specs=[pl.BlockSpec(memory_space=pltpu.SMEM)] + vmem_specs(2),
        out_specs=pl.BlockSpec(memory_space=pltpu.VMEM),
        out_shape=jax.ShapeDtypeStruct((groups, M + 16, query.shape[1]), BF),
        compiler_params=pltpu.CompilerParams(vmem_limit_bytes=VMEM_LIMIT),
        name="pack_queries",
    )(holder, query, valid)


def attend_kernel(sizes, idx, *refs):
    blocks = len(sizes)
    rows, weights = refs[:blocks], refs[blocks : blocks + sum(sizes)]
    total, query, out, keys_values = refs[-4:]
    add_terms(sizes, rows, weights, total, keys_values)
    heads = query.shape[2] // HD
    span = keys_values.shape[0] // ATTEND_SLOTS
    lane = lax.broadcasted_iota(jnp.int32, (M, HD), 1)
    pairs = [(i, h) for i in range(ATTEND_SLOTS) for h in range(heads)]
    places = [idx[blocks + pl.program_id(0) * ATTEND_SLOTS + i] for i in range(ATTEND_SLOTS)]
    scores = {}
    for i, h in pairs:
        cols = slice(h * HD, (h + 1) * HD)
        scores[i, h] = lax.dot_general(
            query[places[i], :M, cols],
            keys_values[i * span : (i + 1) * span, cols],
            (((1,), (1,)), ((), ())),
            preferred_element_type=F32,
        )
    valid = [query[place, M : M + 1, :span].astype(F32) > 0.5 for place in places]
    shares, levels = {}, {}
    for i, h in pairs:
        scaled = jnp.where(valid[i], scores[i, h] * (1.0 / math.sqrt(HD)), -jnp.inf)
        highest = jnp.max(scaled, axis=1, keepdims=True)
        raised = jnp.exp(scaled - highest)
        norm = jnp.sum(raised, axis=1, keepdims=True)
        shares[i, h] = (raised / norm).astype(BF)
        levels[i, h] = highest + jnp.log(norm)
    for i, h in pairs:
        out[places[i], :, h * HD : (h + 1) * HD] = jnp.dot(
            shares[i, h],
            keys_values[i * span : (i + 1) * span, (heads + h) * HD : (heads + h + 1) * HD],
            preferred_element_type=F32,
        ).astype(BF)
    for i in range(ATTEND_SLOTS):
        stats = jnp.zeros((M, HD), F32)
        for h in range(heads):
            first = levels[i, h].astype(BF).astype(F32)
            second = (levels[i, h] - first).astype(BF).astype(F32)
            third = levels[i, h] - first - second
            stats = jnp.where(lane == 3 * h, first, stats)
            stats = jnp.where(lane == 3 * h + 1, second, stats)
            stats = jnp.where(lane == 3 * h + 2, third, stats)
        out[places[i], :, heads * HD :] = stats.astype(BF)


def attend(encoded, pieces, total, owner, query_blocks):
    groups, query_rows, columns = query_blocks.shape
    rows = encoded.shape[0]
    tile = rows // owner.shape[0] * ATTEND_SLOTS
    in_specs, operands = project_operands(encoded, pieces, tile)
    places = jnp.concatenate([jnp.stack([place for place, _ in pieces]).astype(jnp.int32), owner])
    return pl.pallas_call(
        functools.partial(attend_kernel, [len(w) for _, w in pieces]),
        grid_spec=pltpu.PrefetchScalarGridSpec(
            num_scalar_prefetch=1,
            grid=(rows // tile,),
            in_specs=in_specs
            + [
                pl.BlockSpec((tile, 2 * columns), lambda m, i: (m, 0)),
                pl.BlockSpec((groups, query_rows, columns), lambda m, i: (0, 0, 0)),
            ],
            out_specs=pl.BlockSpec((groups, M, columns + HD), lambda m, i: (0, 0, 0)),
            scratch_shapes=[pltpu.VMEM((tile, 2 * columns), BF)],
        ),
        out_shape=jax.ShapeDtypeStruct((groups, M, columns + HD), BF),
        compiler_params=pltpu.CompilerParams(vmem_limit_bytes=VMEM_LIMIT),
        name="attend",
    )(places, *operands, total, query_blocks)


def combine_kernel(holder, parts, out):
    rows, columns = out.shape
    heads = columns // HD
    flat = []
    for u in range(rows // M):
        first, second = parts[holder[2 * u]], parts[holder[2 * u + 1]]
        levels = [part[:, columns:].astype(F32) for part in (first, second)]
        pieces = []
        for h in range(heads):
            cols = slice(h * HD, (h + 1) * HD)
            one, two = [
                level[:, 3 * h : 3 * h + 1]
                + level[:, 3 * h + 1 : 3 * h + 2]
                + level[:, 3 * h + 2 : 3 * h + 3]
                for level in levels
            ]
            top = jnp.maximum(one, two)
            share_one, share_two = jnp.exp(one - top), jnp.exp(two - top)
            both = share_one + share_two
            pieces.append(
                first[:, cols].astype(F32) * (share_one / both)
                + second[:, cols].astype(F32) * (share_two / both)
            )
        flat.append(jnp.concatenate(pieces, axis=1))
    shifted = pltpu.roll(jnp.concatenate(flat, axis=0), M - 1, 0)
    row = lax.broadcasted_iota(jnp.int32, (rows, columns), 0)
    out[...] = jnp.where(row >= M - 1, shifted, 0.0).astype(BF)


def combine(holder, parts, rows):
    columns = parts.shape[2] - HD
    return pl.pallas_call(
        combine_kernel,
        in_specs=[pl.BlockSpec(memory_space=pltpu.SMEM)] + vmem_specs(1),
        out_specs=pl.BlockSpec(memory_space=pltpu.VMEM),
        out_shape=jax.ShapeDtypeStruct((rows, columns), BF),
        compiler_params=pltpu.CompilerParams(vmem_limit_bytes=VMEM_LIMIT),
        name="combine",
    )(holder, parts)


def mix_kernel(place, *refs):
    attended, mine, other, out = refs[:4], refs[4:8], refs[8:12], refs[12]
    core = place[1]
    half = mine[0].shape[0]
    total = None
    for r in range(4):
        for swap, weight in ((0, mine[r]), (1, other[r])):
            cols = pl.ds(pl.multiple_of(((core + swap) % 2) * half, half), half)
            term = jnp.dot(attended[r][:, cols], weight[...], preferred_element_type=F32)
            total = term if total is None else total + term
    out[...] = total.astype(out.dtype)


def mix(place, attended, mine, other, kind):
    rows, columns = attended[0].shape
    half, width = mine[0].shape[0], mine[0].shape[1] // 2
    tile = width // 2
    weight_spec = pl.BlockSpec((half, tile), lambda j, place: (0, place[0] * 2 + j))
    return pl.pallas_call(
        mix_kernel,
        grid_spec=pltpu.PrefetchScalarGridSpec(
            num_scalar_prefetch=1,
            grid=(2,),
            in_specs=[pl.BlockSpec((rows, columns), lambda j, place: (0, 0))] * 4
            + [weight_spec] * 8,
            out_specs=pl.BlockSpec((rows, tile), lambda j, place: (0, j)),
        ),
        out_shape=jax.ShapeDtypeStruct((rows, width), kind),
        compiler_params=pltpu.CompilerParams(vmem_limit_bytes=VMEM_LIMIT),
        cost_estimate=pl.CostEstimate(
            flops=8 * rows * columns * width, bytes_accessed=8 * columns * width, transcendentals=0
        ),
        name="mix",
    )(place, *attended, *mine, *other)


def body(encoded_neighbours, kv_weight, queries, out_weight, neighbour_ids, slot_map):
    groups = lax.axis_size("dp")
    position = lax.axis_index("dp")
    tensor_at = lax.axis_index("tensor")
    z, y, core = position // 4, (position // 2) % 2, position % 2
    x, y_lo = tensor_at // 2, tensor_at % 2
    slot_count, span, model_width = encoded_neighbours.shape
    encoded = encoded_neighbours.reshape(slot_count * span, model_width)
    held = lax.dynamic_slice_in_dim(slot_map, position * slot_count, slot_count)
    owner = held // slot_count
    wanted = position * slot_count + jnp.arange(slot_count, dtype=jnp.int32)
    holder = (
        jnp.sum(
            jnp.where(
                slot_map[None, :] == wanted[:, None],
                jnp.arange(slot_map.shape[0], dtype=jnp.int32)[None, :],
                0,
            ),
            axis=1,
        )
        // slot_count
    )
    valid = (neighbour_ids.reshape(slot_count, span) != 0).astype(F32)

    def send(block, pairs):
        return lax.ppermute(block, "dp", pairs)

    def across_x(block, step):
        return lax.ppermute(block, "tensor", tensor_pairs(step, 0))

    def with_twin(dz, dy, *arrays):
        def at(dc):
            return ((z + dz) % 4) * 4 + ((y + dy) % 2) * 2 + (core + dc) % 2

        return [(at(0), arrays), (at(1), tuple(send(array, CORE_SWAP) for array in arrays))]

    own = kv_weight
    below, above, across = send(own, Z_UP), send(own, Z_DOWN), send(own, Y_SWAP)
    mix_own, to_next, to_last, to_far = split_rows(
        core, [x, (x + 1) % 4, (x + 3) % 4, (x + 2) % 4], out_weight
    )
    total = project(encoded, with_twin(0, 0, own), None)
    below, above, across, total, to_next = lax.optimization_barrier(
        (below, above, across, total, to_next)
    )

    far, across_below, across_above = send(above, Z_DOWN), send(across, Z_UP), send(above, Y_SWAP)
    mix_last = across_x(to_next, 1)
    total = project(
        encoded,
        with_twin(-1, 0, below) + with_twin(1, 0, above) + with_twin(0, 1, across),
        total,
    )
    total, late_holder = lax.optimization_barrier((total, holder))
    outgoing = pack_queries(queries, valid, late_holder, groups)
    query_blocks = lax.all_to_all(outgoing, "dp", 0, 0, tiled=True)
    far, across_below, across_above, total, mix_last, to_last, outgoing = lax.optimization_barrier(
        (far, across_below, across_above, total, mix_last, to_last, outgoing)
    )

    far_keys, far_values = send(across_below[:1], Z_UP), send(across_above[1:], Z_DOWN)
    mix_next = across_x(to_last, -1)
    total = project(
        encoded,
        with_twin(2, 0, far) + with_twin(-1, 1, across_below) + with_twin(1, 1, across_above),
        total,
    )
    far_keys, far_values, total, mix_next, to_far = lax.optimization_barrier(
        (far_keys, far_values, total, mix_next, to_far)
    )

    mix_far = across_x(to_far, 2)
    parts = attend(encoded, with_twin(2, 1, far_keys, far_values), total, owner, query_blocks)
    returned = lax.all_to_all(parts, "dp", 0, 0, tiled=True)
    attended = combine(holder, returned, queries.shape[0])

    near = [attended, across_x(attended, 1), across_x(attended, -1), across_x(attended, 2)]
    mine = [mix_own, mix_last, mix_next, mix_far]
    other = [send(block, CORE_SWAP) for block in mine]
    theirs = mix(jnp.stack([1 - y_lo, core]), near, mine, other, BF)
    arrived = lax.ppermute(theirs, "tensor", tensor_pairs(0, 1))
    ours = mix(jnp.stack([y_lo, core]), near, mine, other, F32)
    return (ours + arrived.astype(F32)).astype(BF)


def solution(mesh):
    placed = (
        P("dp", None, None),
        P(None, "dp", "tensor"),
        P("dp", "tensor"),
        P("tensor", None),
        P("dp", None, None, None),
        P(),
    )
    return jax.shard_map(
        body, mesh=mesh, in_specs=placed, out_specs=P("dp", "tensor"), check_vma=False
    )
```

```python
import functools
import math

import jax
import jax.numpy as jnp
from jax import lax
from jax.experimental import pallas as pl
from jax.experimental.pallas import tpu as pltpu
from jax.sharding import PartitionSpec as P

HD = 128
M = 64
BF = jnp.bfloat16
F32 = jnp.float32
ATTEND_SLOTS = 2
VMEM_LIMIT = 48 * 1024 * 1024


def dp_pairs(dz, dy, dc):
    pairs = []
    for i in range(16):
        z, y, c = i // 4, (i // 2) % 2, i % 2
        pairs.append((i, ((z + dz) % 4) * 4 + ((y + dy) % 2) * 2 + (c + dc) % 2))
    return pairs


def tensor_pairs(dx, dy):
    pairs = []
    for i in range(8):
        x, y = i // 2, i % 2
        pairs.append((i, ((x + dx) % 4) * 2 + (y + dy) % 2))
    return pairs


Z_UP, Z_DOWN = dp_pairs(1, 0, 0), dp_pairs(-1, 0, 0)
Y_SWAP, CORE_SWAP = dp_pairs(0, 1, 0), dp_pairs(0, 0, 1)


def vmem_specs(count):
    return [pl.BlockSpec(memory_space=pltpu.VMEM)] * count


def add_terms(sizes, rows, weight_refs, total, out):
    weights = []
    at = 0
    for size in sizes:
        if size == 1:
            weights.append((weight_refs[at].at[0], weight_refs[at].at[1]))
        else:
            weights.append((weight_refs[at].at[0], weight_refs[at + 1].at[0]))
        at += size
    columns = out.shape[1] // 2
    for side in range(2):
        cols = slice(side * columns, (side + 1) * columns)
        value = None if total is None else total[:, cols]
        for row, weight in zip(rows, weights):
            term = jnp.dot(row[...], weight[side][...], preferred_element_type=F32)
            value = term if value is None else value + term
        out[:, cols] = value.astype(out.dtype)


def project_kernel(sizes, has_total, idx, *refs):
    del idx
    blocks = len(sizes)
    rows, weights = refs[:blocks], refs[blocks : blocks + sum(sizes)]
    add_terms(sizes, rows, weights, refs[-2] if has_total else None, refs[-1])


def project_operands(encoded, pieces, tile):
    arrays = [array for _, weight in pieces for array in weight]
    depth = arrays[0].shape[1]
    specs = [
        pl.BlockSpec((tile, depth), lambda m, i, j=j: (m, i[j])) for j in range(len(pieces))
    ] + [
        pl.BlockSpec(array.shape, lambda m, i: (0, 0, 0), pipeline_mode=pl.Buffered(1))
        for array in arrays
    ]
    return specs, [encoded] * len(pieces) + arrays


def project(encoded, pieces, total):
    rows = encoded.shape[0]
    depth, columns = pieces[0][1][0].shape[1:]
    tile = 256
    in_specs, operands = project_operands(encoded, pieces, tile)
    total_spec = pl.BlockSpec((tile, 2 * columns), lambda m, i: (m, 0))
    if total is not None:
        in_specs.append(total_spec)
        operands.append(total)
    return pl.pallas_call(
        functools.partial(project_kernel, [len(w) for _, w in pieces], total is not None),
        grid_spec=pltpu.PrefetchScalarGridSpec(
            num_scalar_prefetch=1, grid=(rows // tile,), in_specs=in_specs, out_specs=total_spec
        ),
        out_shape=jax.ShapeDtypeStruct((rows, 2 * columns), F32),
        compiler_params=pltpu.CompilerParams(vmem_limit_bytes=VMEM_LIMIT),
        cost_estimate=pl.CostEstimate(
            flops=4 * rows * depth * columns * len(pieces),
            bytes_accessed=2 * len(pieces) * depth * (rows + 2 * columns),
            transcendentals=0,
        ),
        name="project",
    )(jnp.stack([place for place, _ in pieces]).astype(jnp.int32), *operands)


def split_kernel(place, *refs):
    del place
    count = len(refs) // 2
    for source, target in zip(refs[:count], refs[count:]):
        target[...] = source[...]


def split_rows(core, places, weight):
    parts = len(places)
    half, width = weight.shape[0] // 2, weight.shape[1] // parts
    tile = half // 4
    return pl.pallas_call(
        split_kernel,
        grid_spec=pltpu.PrefetchScalarGridSpec(
            num_scalar_prefetch=1,
            grid=(4,),
            in_specs=[
                pl.BlockSpec((tile, width), lambda m, place, r=r: (place[parts] * 4 + m, place[r]))
                for r in range(parts)
            ],
            out_specs=[pl.BlockSpec((tile, width), lambda m, place: (m, 0))] * parts,
        ),
        out_shape=[jax.ShapeDtypeStruct((half, width), weight.dtype)] * parts,
        compiler_params=pltpu.CompilerParams(vmem_limit_bytes=VMEM_LIMIT),
        cost_estimate=pl.CostEstimate(
            flops=0, bytes_accessed=half * width // 8, transcendentals=0
        ),
        name="split_rows",
    )(jnp.stack(places + [core]), *[weight] * parts)


def pack_kernel(holder, query, valid, out):
    rows = query.shape[0]
    shifted = pltpu.roll(query[...].astype(F32), rows - (M - 1), 0).astype(BF)
    heads = query.shape[1] // HD
    for j in range(valid.shape[0]):
        u = j // 2
        for h in range(heads):
            out[holder[j], h * M : (h + 1) * M, :] = shifted[
                u * M : (u + 1) * M, h * HD : (h + 1) * HD
            ]
        out[holder[j], heads * M :, :] = jnp.tile(valid[j : j + 1, :], (16, 1)).astype(BF)


def pack_queries(query, valid, holder, groups):
    return pl.pallas_call(
        pack_kernel,
        in_specs=[pl.BlockSpec(memory_space=pltpu.SMEM)] + vmem_specs(2),
        out_specs=pl.BlockSpec(memory_space=pltpu.VMEM),
        out_shape=jax.ShapeDtypeStruct((groups, query.shape[1] // HD * M + 16, HD), BF),
        compiler_params=pltpu.CompilerParams(vmem_limit_bytes=VMEM_LIMIT),
        name="pack_queries",
    )(holder, query, valid)


def attend_kernel(sizes, idx, *refs):
    blocks = len(sizes)
    rows, weights = refs[:blocks], refs[blocks : blocks + sum(sizes)]
    total, query, out, keys_values = refs[-4:]
    add_terms(sizes, rows, weights, total, keys_values)
    heads = keys_values.shape[1] // (2 * HD)
    span = keys_values.shape[0] // ATTEND_SLOTS
    lane = lax.broadcasted_iota(jnp.int32, (M, HD), 1)
    pairs = [(i, h) for i in range(ATTEND_SLOTS) for h in range(heads)]
    places = [idx[blocks + pl.program_id(0) * ATTEND_SLOTS + i] for i in range(ATTEND_SLOTS)]
    scores = {}
    for i, h in pairs:
        cols = slice(h * HD, (h + 1) * HD)
        scores[i, h] = lax.dot_general(
            query[places[i], h * M : (h + 1) * M, :],
            keys_values[i * span : (i + 1) * span, cols],
            (((1,), (1,)), ((), ())),
            preferred_element_type=F32,
        )
    valid = [query[place, heads * M : heads * M + 1, :span].astype(F32) > 0.5 for place in places]
    shares, levels = {}, {}
    for i, h in pairs:
        scaled = jnp.where(valid[i], scores[i, h] * (1.0 / math.sqrt(HD)), -jnp.inf)
        highest = jnp.max(scaled, axis=1, keepdims=True)
        raised = jnp.exp(scaled - highest)
        norm = jnp.sum(raised, axis=1, keepdims=True)
        shares[i, h] = (raised / norm).astype(BF)
        levels[i, h] = highest + jnp.log(norm)
    for i, h in pairs:
        out[places[i], h * M : (h + 1) * M, :] = jnp.dot(
            shares[i, h],
            keys_values[i * span : (i + 1) * span, (heads + h) * HD : (heads + h + 1) * HD],
            preferred_element_type=F32,
        ).astype(BF)
    for i in range(ATTEND_SLOTS):
        stats = jnp.zeros((M, HD), F32)
        for h in range(heads):
            first = levels[i, h].astype(BF).astype(F32)
            second = (levels[i, h] - first).astype(BF).astype(F32)
            third = levels[i, h] - first - second
            stats = jnp.where(lane == h, first, stats)
            stats = jnp.where(lane == heads + h, second, stats)
            stats = jnp.where(lane == 2 * heads + h, third, stats)
        square = jnp.concatenate([stats, jnp.zeros((HD - M, HD), F32)], axis=0)
        out[places[i], heads * M :, :] = square.T[:16].astype(BF)


def attend(encoded, pieces, total, owner, query_blocks):
    rows = encoded.shape[0]
    tile = rows // owner.shape[0] * ATTEND_SLOTS
    in_specs, operands = project_operands(encoded, pieces, tile)
    places = jnp.concatenate([jnp.stack([place for place, _ in pieces]).astype(jnp.int32), owner])
    return pl.pallas_call(
        functools.partial(attend_kernel, [len(w) for _, w in pieces]),
        grid_spec=pltpu.PrefetchScalarGridSpec(
            num_scalar_prefetch=1,
            grid=(rows // tile,),
            in_specs=in_specs
            + [
                pl.BlockSpec((tile, total.shape[1]), lambda m, i: (m, 0)),
                pl.BlockSpec(query_blocks.shape, lambda m, i: (0, 0, 0)),
            ],
            out_specs=pl.BlockSpec(query_blocks.shape, lambda m, i: (0, 0, 0)),
            scratch_shapes=[pltpu.VMEM((tile, total.shape[1]), BF)],
        ),
        out_shape=jax.ShapeDtypeStruct(query_blocks.shape, BF),
        compiler_params=pltpu.CompilerParams(vmem_limit_bytes=VMEM_LIMIT),
        name="attend",
    )(places, *operands, total, query_blocks)


def combine_kernel(holder, parts, out):
    rows, columns = out.shape
    heads, stretches = columns // HD, rows // M
    shares = []
    for u in range(stretches):
        levels = []
        for n in range(2):
            stats = parts[holder[2 * u + n], heads * M :, :].astype(F32)
            levels.append(stats[:heads] + stats[heads : 2 * heads] + stats[2 * heads : 3 * heads])
        top = jnp.maximum(levels[0], levels[1])
        raised = [jnp.exp(level - top) for level in levels]
        both = raised[0] + raised[1]
        shares += [raised[0] / both, raised[1] / both]
    used = 2 * stretches * heads
    share_columns = jnp.concatenate(shares + [jnp.zeros((HD - used, HD), F32)], axis=0).T
    flat = []
    for u in range(stretches):
        pieces = []
        for h in range(heads):
            terms = []
            for n in range(2):
                at = (2 * u + n) * heads + h
                part = parts[holder[2 * u + n], h * M : (h + 1) * M, :].astype(F32)
                terms.append(part * share_columns[:M, at : at + 1])
            pieces.append(terms[0] + terms[1])
        flat.append(jnp.concatenate(pieces, axis=1))
    shifted = pltpu.roll(jnp.concatenate(flat, axis=0), M - 1, 0)
    row = lax.broadcasted_iota(jnp.int32, (rows, columns), 0)
    out[...] = jnp.where(row >= M - 1, shifted, 0.0).astype(BF)


def combine(holder, parts, rows, columns):
    return pl.pallas_call(
        combine_kernel,
        in_specs=[pl.BlockSpec(memory_space=pltpu.SMEM)] + vmem_specs(1),
        out_specs=pl.BlockSpec(memory_space=pltpu.VMEM),
        out_shape=jax.ShapeDtypeStruct((rows, columns), BF),
        compiler_params=pltpu.CompilerParams(vmem_limit_bytes=VMEM_LIMIT),
        name="combine",
    )(holder, parts)


def mix_kernel(place, *refs):
    attended, mine, other, out = refs[:4], refs[4:8], refs[8:12], refs[12]
    core = place[1]
    half = mine[0].shape[0]
    total = None
    for r in range(4):
        for swap, weight in ((0, mine[r]), (1, other[r])):
            cols = pl.ds(pl.multiple_of(((core + swap) % 2) * half, half), half)
            term = jnp.dot(attended[r][:, cols], weight[...], preferred_element_type=F32)
            total = term if total is None else total + term
    out[...] = total.astype(out.dtype)


def mix(place, attended, mine, other, kind):
    rows, columns = attended[0].shape
    half, width = mine[0].shape[0], mine[0].shape[1] // 2
    tile = width // 2
    weight_spec = pl.BlockSpec((half, tile), lambda j, place: (0, place[0] * 2 + j))
    return pl.pallas_call(
        mix_kernel,
        grid_spec=pltpu.PrefetchScalarGridSpec(
            num_scalar_prefetch=1,
            grid=(2,),
            in_specs=[pl.BlockSpec((rows, columns), lambda j, place: (0, 0))] * 4
            + [weight_spec] * 8,
            out_specs=pl.BlockSpec((rows, tile), lambda j, place: (0, j)),
        ),
        out_shape=jax.ShapeDtypeStruct((rows, width), kind),
        compiler_params=pltpu.CompilerParams(vmem_limit_bytes=VMEM_LIMIT),
        cost_estimate=pl.CostEstimate(
            flops=8 * rows * columns * width, bytes_accessed=8 * columns * width, transcendentals=0
        ),
        name="mix",
    )(place, *attended, *mine, *other)


def body(encoded_neighbours, kv_weight, queries, out_weight, neighbour_ids, slot_map):
    groups = lax.axis_size("dp")
    position = lax.axis_index("dp")
    tensor_at = lax.axis_index("tensor")
    z, y, core = position // 4, (position // 2) % 2, position % 2
    x, y_lo = tensor_at // 2, tensor_at % 2
    slot_count, span, model_width = encoded_neighbours.shape
    encoded = encoded_neighbours.reshape(slot_count * span, model_width)
    held = lax.dynamic_slice_in_dim(slot_map, position * slot_count, slot_count)
    owner = held // slot_count
    wanted = position * slot_count + jnp.arange(slot_count, dtype=jnp.int32)
    holder = (
        jnp.sum(
            jnp.where(
                slot_map[None, :] == wanted[:, None],
                jnp.arange(slot_map.shape[0], dtype=jnp.int32)[None, :],
                0,
            ),
            axis=1,
        )
        // slot_count
    )
    valid = (neighbour_ids.reshape(slot_count, span) != 0).astype(F32)

    def send(block, pairs):
        return lax.ppermute(block, "dp", pairs)

    def across_x(block, step):
        return lax.ppermute(block, "tensor", tensor_pairs(step, 0))

    def with_twin(dz, dy, *arrays):
        def at(dc):
            return ((z + dz) % 4) * 4 + ((y + dy) % 2) * 2 + (core + dc) % 2

        return [(at(0), arrays), (at(1), tuple(send(array, CORE_SWAP) for array in arrays))]

    own = kv_weight
    below, above, across = send(own, Z_UP), send(own, Z_DOWN), send(own, Y_SWAP)
    mix_own, to_next, to_last, to_far = split_rows(
        core, [x, (x + 1) % 4, (x + 3) % 4, (x + 2) % 4], out_weight
    )
    total = project(encoded, with_twin(0, 0, own), None)
    below, above, across, total, to_next = lax.optimization_barrier(
        (below, above, across, total, to_next)
    )

    far, across_below, across_above = send(above, Z_DOWN), send(across, Z_UP), send(above, Y_SWAP)
    mix_last = across_x(to_next, 1)
    total = project(
        encoded,
        with_twin(-1, 0, below) + with_twin(1, 0, above) + with_twin(0, 1, across),
        total,
    )
    total, late_holder = lax.optimization_barrier((total, holder))
    outgoing = pack_queries(queries, valid, late_holder, groups)
    query_blocks = lax.all_to_all(outgoing, "dp", 0, 0, tiled=True)
    far, across_below, across_above, total, mix_last, to_last, outgoing = lax.optimization_barrier(
        (far, across_below, across_above, total, mix_last, to_last, outgoing)
    )

    far_keys, far_values = send(across_below[:1], Z_UP), send(across_above[1:], Z_DOWN)
    mix_next = across_x(to_last, -1)
    total = project(
        encoded,
        with_twin(2, 0, far) + with_twin(-1, 1, across_below) + with_twin(1, 1, across_above),
        total,
    )
    far_keys, far_values, total, mix_next, to_far, query_blocks = lax.optimization_barrier(
        (far_keys, far_values, total, mix_next, to_far, query_blocks)
    )

    mix_far = across_x(to_far, 2)
    parts = attend(encoded, with_twin(2, 1, far_keys, far_values), total, owner, query_blocks)
    returned = lax.all_to_all(parts, "dp", 0, 0, tiled=True)
    attended = combine(holder, returned, *queries.shape)

    near = [attended, across_x(attended, 1), across_x(attended, -1), across_x(attended, 2)]
    mine = [mix_own, mix_last, mix_next, mix_far]
    other = [send(block, CORE_SWAP) for block in mine]
    theirs = mix(jnp.stack([1 - y_lo, core]), near, mine, other, BF)
    arrived = lax.ppermute(theirs, "tensor", tensor_pairs(0, 1))
    ours = mix(jnp.stack([y_lo, core]), near, mine, other, F32)
    return (ours + arrived.astype(F32)).astype(BF)


def solution(mesh):
    placed = (
        P("dp", None, None),
        P(None, "dp", "tensor"),
        P("dp", "tensor"),
        P("tensor", None),
        P("dp", None, None, None),
        P(),
    )
    return jax.shard_map(
        body, mesh=mesh, in_specs=placed, out_specs=P("dp", "tensor"), check_vma=False
    )
```

```python
import functools
import math

import jax
import jax.numpy as jnp
from jax import lax
from jax.experimental import pallas as pl
from jax.experimental.pallas import tpu as pltpu
from jax.sharding import PartitionSpec as P

HD = 128
M = 64
BF = jnp.bfloat16
F32 = jnp.float32
ATTEND_SLOTS = 2
VMEM_LIMIT = 48 * 1024 * 1024


def dp_pairs(dz, dy, dc):
    pairs = []
    for i in range(16):
        z, y, c = i // 4, (i // 2) % 2, i % 2
        pairs.append((i, ((z + dz) % 4) * 4 + ((y + dy) % 2) * 2 + (c + dc) % 2))
    return pairs


def tensor_pairs(dx, dy):
    pairs = []
    for i in range(8):
        x, y = i // 2, i % 2
        pairs.append((i, ((x + dx) % 4) * 2 + (y + dy) % 2))
    return pairs


Z_UP, Z_DOWN = dp_pairs(1, 0, 0), dp_pairs(-1, 0, 0)
Y_SWAP, CORE_SWAP = dp_pairs(0, 1, 0), dp_pairs(0, 0, 1)


def vmem_specs(count):
    return [pl.BlockSpec(memory_space=pltpu.VMEM)] * count


def add_terms(sizes, rows, weight_refs, total, out):
    weights = []
    at = 0
    for size in sizes:
        if size == 1:
            weights.append((weight_refs[at].at[0], weight_refs[at].at[1]))
        else:
            weights.append((weight_refs[at].at[0], weight_refs[at + 1].at[0]))
        at += size
    columns = out.shape[1] // 2
    for side in range(2):
        cols = slice(side * columns, (side + 1) * columns)
        value = None if total is None else total[:, cols]
        for row, weight in zip(rows, weights):
            term = jnp.dot(row[...], weight[side][...], preferred_element_type=F32)
            value = term if value is None else value + term
        out[:, cols] = value.astype(out.dtype)


def project_kernel(sizes, has_total, idx, *refs):
    del idx
    blocks = len(sizes)
    rows, weights = refs[:blocks], refs[blocks : blocks + sum(sizes)]
    add_terms(sizes, rows, weights, refs[-2] if has_total else None, refs[-1])


def project_operands(encoded, pieces, tile):
    arrays = [array for _, weight in pieces for array in weight]
    depth = arrays[0].shape[1]
    specs = [
        pl.BlockSpec((tile, depth), lambda m, i, j=j: (m, i[j])) for j in range(len(pieces))
    ] + [
        pl.BlockSpec(array.shape, lambda m, i: (0, 0, 0), pipeline_mode=pl.Buffered(1))
        for array in arrays
    ]
    return specs, [encoded] * len(pieces) + arrays


def project(encoded, pieces, total):
    rows = encoded.shape[0]
    depth, columns = pieces[0][1][0].shape[1:]
    tile = 256
    in_specs, operands = project_operands(encoded, pieces, tile)
    total_spec = pl.BlockSpec((tile, 2 * columns), lambda m, i: (m, 0))
    if total is not None:
        in_specs.append(total_spec)
        operands.append(total)
    return pl.pallas_call(
        functools.partial(project_kernel, [len(w) for _, w in pieces], total is not None),
        grid_spec=pltpu.PrefetchScalarGridSpec(
            num_scalar_prefetch=1, grid=(rows // tile,), in_specs=in_specs, out_specs=total_spec
        ),
        out_shape=jax.ShapeDtypeStruct((rows, 2 * columns), F32),
        compiler_params=pltpu.CompilerParams(vmem_limit_bytes=VMEM_LIMIT),
        cost_estimate=pl.CostEstimate(
            flops=4 * rows * depth * columns * len(pieces),
            bytes_accessed=2 * len(pieces) * depth * (rows + 2 * columns),
            transcendentals=0,
        ),
        name="project",
    )(jnp.stack([place for place, _ in pieces]).astype(jnp.int32), *operands)


def split_kernel(place, *refs):
    del place
    count = len(refs) // 2
    for source, target in zip(refs[:count], refs[count:]):
        target[...] = source[...]


def split_rows(core, places, weight):
    parts = len(places)
    half, width = weight.shape[0] // 2, weight.shape[1] // parts
    tile = half // 4
    return pl.pallas_call(
        split_kernel,
        grid_spec=pltpu.PrefetchScalarGridSpec(
            num_scalar_prefetch=1,
            grid=(4,),
            in_specs=[
                pl.BlockSpec((tile, width), lambda m, place, r=r: (place[parts] * 4 + m, place[r]))
                for r in range(parts)
            ],
            out_specs=[pl.BlockSpec((tile, width), lambda m, place: (m, 0))] * parts,
        ),
        out_shape=[jax.ShapeDtypeStruct((half, width), weight.dtype)] * parts,
        compiler_params=pltpu.CompilerParams(vmem_limit_bytes=VMEM_LIMIT),
        cost_estimate=pl.CostEstimate(
            flops=0, bytes_accessed=half * width // 8, transcendentals=0
        ),
        name="split_rows",
    )(jnp.stack(places + [core]), *[weight] * parts)


def pack_kernel(holder, query, valid, out):
    rows = query.shape[0]
    shifted = pltpu.roll(query[...].astype(F32), rows - (M - 1), 0).astype(BF)
    heads = query.shape[1] // HD
    for j in range(valid.shape[0]):
        u = j // 2
        for h in range(heads):
            out[holder[j], h * M : (h + 1) * M, :] = shifted[
                u * M : (u + 1) * M, h * HD : (h + 1) * HD
            ]
        out[holder[j], heads * M :, :] = jnp.tile(valid[j : j + 1, :], (16, 1)).astype(BF)


def pack_queries(query, valid, holder, groups):
    return pl.pallas_call(
        pack_kernel,
        in_specs=[pl.BlockSpec(memory_space=pltpu.SMEM)] + vmem_specs(2),
        out_specs=pl.BlockSpec(memory_space=pltpu.VMEM),
        out_shape=jax.ShapeDtypeStruct((groups, query.shape[1] // HD * M + 16, HD), BF),
        compiler_params=pltpu.CompilerParams(vmem_limit_bytes=VMEM_LIMIT),
        name="pack_queries",
    )(holder, query, valid)


def attend_kernel(sizes, idx, *refs):
    blocks = len(sizes)
    rows, weights = refs[:blocks], refs[blocks : blocks + sum(sizes)]
    total, query, out, keys_values = refs[-4:]
    add_terms(sizes, rows, weights, total, keys_values)
    heads = keys_values.shape[1] // (2 * HD)
    span = keys_values.shape[0] // ATTEND_SLOTS
    lane = lax.broadcasted_iota(jnp.int32, (M, HD), 1)
    pairs = [(i, h) for i in range(ATTEND_SLOTS) for h in range(heads)]
    places = [idx[blocks + pl.program_id(0) * ATTEND_SLOTS + i] for i in range(ATTEND_SLOTS)]
    scores = {}
    for i, h in pairs:
        cols = slice(h * HD, (h + 1) * HD)
        scores[i, h] = lax.dot_general(
            query[places[i], h * M : (h + 1) * M, :],
            keys_values[i * span : (i + 1) * span, cols],
            (((1,), (1,)), ((), ())),
            preferred_element_type=F32,
        )
    valid = [query[place, heads * M : heads * M + 1, :span].astype(F32) > 0.5 for place in places]
    shares, levels = {}, {}
    for i, h in pairs:
        scaled = jnp.where(valid[i], scores[i, h] * (1.0 / math.sqrt(HD)), -jnp.inf)
        highest = jnp.max(scaled, axis=1, keepdims=True)
        raised = jnp.exp(scaled - highest)
        norm = jnp.sum(raised, axis=1, keepdims=True)
        shares[i, h] = (raised / norm).astype(BF)
        levels[i, h] = highest + jnp.log(norm)
    for i, h in pairs:
        out[places[i], h * M : (h + 1) * M, :] = jnp.dot(
            shares[i, h],
            keys_values[i * span : (i + 1) * span, (heads + h) * HD : (heads + h + 1) * HD],
            preferred_element_type=F32,
        ).astype(BF)
    for i in range(ATTEND_SLOTS):
        stats = jnp.zeros((M, HD), F32)
        for h in range(heads):
            first = levels[i, h].astype(BF).astype(F32)
            second = (levels[i, h] - first).astype(BF).astype(F32)
            third = levels[i, h] - first - second
            stats = jnp.where(lane == h, first, stats)
            stats = jnp.where(lane == heads + h, second, stats)
            stats = jnp.where(lane == 2 * heads + h, third, stats)
        square = jnp.concatenate([stats, jnp.zeros((HD - M, HD), F32)], axis=0)
        out[places[i], heads * M :, :] = square.T[:16].astype(BF)


def attend(encoded, pieces, total, owner, query_blocks):
    rows = encoded.shape[0]
    tile = rows // owner.shape[0] * ATTEND_SLOTS
    in_specs, operands = project_operands(encoded, pieces, tile)
    places = jnp.concatenate([jnp.stack([place for place, _ in pieces]).astype(jnp.int32), owner])
    return pl.pallas_call(
        functools.partial(attend_kernel, [len(w) for _, w in pieces]),
        grid_spec=pltpu.PrefetchScalarGridSpec(
            num_scalar_prefetch=1,
            grid=(rows // tile,),
            in_specs=in_specs
            + [
                pl.BlockSpec((tile, total.shape[1]), lambda m, i: (m, 0)),
                pl.BlockSpec(query_blocks.shape, lambda m, i: (0, 0, 0)),
            ],
            out_specs=pl.BlockSpec(query_blocks.shape, lambda m, i: (0, 0, 0)),
            scratch_shapes=[pltpu.VMEM((tile, total.shape[1]), BF)],
        ),
        out_shape=jax.ShapeDtypeStruct(query_blocks.shape, BF),
        compiler_params=pltpu.CompilerParams(vmem_limit_bytes=VMEM_LIMIT),
        name="attend",
    )(places, *operands, total, query_blocks)


def combine_kernel(lead, holder, parts, out):
    rows, columns = out.shape[0] + lead, out.shape[1]
    heads, stretches = columns // HD, rows // M
    shares = []
    for u in range(stretches):
        levels = []
        for n in range(2):
            stats = parts[holder[2 * u + n], heads * M :, :].astype(F32)
            levels.append(stats[:heads] + stats[heads : 2 * heads] + stats[2 * heads : 3 * heads])
        top = jnp.maximum(levels[0], levels[1])
        raised = [jnp.exp(level - top) for level in levels]
        both = raised[0] + raised[1]
        shares += [raised[0] / both, raised[1] / both]
    used = 2 * stretches * heads
    share_columns = jnp.concatenate(shares + [jnp.zeros((HD - used, HD), F32)], axis=0).T
    flat = []
    for u in range(stretches):
        pieces = []
        for h in range(heads):
            terms = []
            for n in range(2):
                at = (2 * u + n) * heads + h
                part = parts[holder[2 * u + n], h * M : (h + 1) * M, :].astype(F32)
                terms.append(part * share_columns[:M, at : at + 1])
            pieces.append(terms[0] + terms[1])
        flat.append(jnp.concatenate(pieces, axis=1))
    shifted = pltpu.roll(jnp.concatenate(flat, axis=0), M - 1, 0)
    row = lax.broadcasted_iota(jnp.int32, (rows, columns), 0)
    out[...] = jnp.where(row >= M - 1, shifted, 0.0)[lead:].astype(BF)


def combine(holder, parts, rows, columns, lead):
    return pl.pallas_call(
        functools.partial(combine_kernel, lead),
        in_specs=[pl.BlockSpec(memory_space=pltpu.SMEM)] + vmem_specs(1),
        out_specs=pl.BlockSpec(memory_space=pltpu.VMEM),
        out_shape=jax.ShapeDtypeStruct((rows - lead, columns), BF),
        compiler_params=pltpu.CompilerParams(vmem_limit_bytes=VMEM_LIMIT),
        name="combine",
    )(holder, parts)


def mix_kernel(place, *refs):
    attended, mine, other, out = refs[:4], refs[4:8], refs[8:12], refs[12]
    core = place[1]
    half = mine[0].shape[0]
    total = None
    for r in range(4):
        for swap, weight in ((0, mine[r]), (1, other[r])):
            cols = pl.ds(pl.multiple_of(((core + swap) % 2) * half, half), half)
            term = jnp.dot(attended[r][:, cols], weight[...], preferred_element_type=F32)
            total = term if total is None else total + term
    out[...] = total.astype(out.dtype)


def mix(place, attended, mine, other, kind):
    rows, columns = attended[0].shape
    half, width = mine[0].shape[0], mine[0].shape[1] // 2
    tile = width // 2
    weight_spec = pl.BlockSpec((half, tile), lambda j, place: (0, place[0] * 2 + j))
    return pl.pallas_call(
        mix_kernel,
        grid_spec=pltpu.PrefetchScalarGridSpec(
            num_scalar_prefetch=1,
            grid=(2,),
            in_specs=[pl.BlockSpec((rows, columns), lambda j, place: (0, 0))] * 4
            + [weight_spec] * 8,
            out_specs=pl.BlockSpec((rows, tile), lambda j, place: (0, j)),
        ),
        out_shape=jax.ShapeDtypeStruct((rows, width), kind),
        compiler_params=pltpu.CompilerParams(vmem_limit_bytes=VMEM_LIMIT),
        cost_estimate=pl.CostEstimate(
            flops=8 * rows * columns * width, bytes_accessed=8 * columns * width, transcendentals=0
        ),
        name="mix",
    )(place, *attended, *mine, *other)


def body(encoded_neighbours, kv_weight, queries, out_weight, neighbour_ids, slot_map):
    groups = lax.axis_size("dp")
    position = lax.axis_index("dp")
    tensor_at = lax.axis_index("tensor")
    z, y, core = position // 4, (position // 2) % 2, position % 2
    x, y_lo = tensor_at // 2, tensor_at % 2
    slot_count, span, model_width = encoded_neighbours.shape
    encoded = encoded_neighbours.reshape(slot_count * span, model_width)
    held = lax.dynamic_slice_in_dim(slot_map, position * slot_count, slot_count)
    owner = held // slot_count
    wanted = position * slot_count + jnp.arange(slot_count, dtype=jnp.int32)
    holder = (
        jnp.sum(
            jnp.where(
                slot_map[None, :] == wanted[:, None],
                jnp.arange(slot_map.shape[0], dtype=jnp.int32)[None, :],
                0,
            ),
            axis=1,
        )
        // slot_count
    )
    valid = (neighbour_ids.reshape(slot_count, span) != 0).astype(F32)

    def send(block, pairs):
        return lax.ppermute(block, "dp", pairs)

    def across_x(block, step):
        return lax.ppermute(block, "tensor", tensor_pairs(step, 0))

    def with_twin(dz, dy, *arrays):
        def at(dc):
            return ((z + dz) % 4) * 4 + ((y + dy) % 2) * 2 + (core + dc) % 2

        return [(at(0), arrays), (at(1), tuple(send(array, CORE_SWAP) for array in arrays))]

    own = kv_weight
    below, above, across = send(own, Z_UP), send(own, Z_DOWN), send(own, Y_SWAP)
    mix_own, to_next, to_last, to_far = split_rows(
        core, [x, (x + 1) % 4, (x + 3) % 4, (x + 2) % 4], out_weight
    )
    total = project(encoded, with_twin(0, 0, own), None)
    below, above, across, total, to_next = lax.optimization_barrier(
        (below, above, across, total, to_next)
    )

    far, across_below, across_above = send(above, Z_DOWN), send(across, Z_UP), send(above, Y_SWAP)
    mix_last = across_x(to_next, 1)
    total = project(
        encoded,
        with_twin(-1, 0, below) + with_twin(1, 0, above) + with_twin(0, 1, across),
        total,
    )
    total, late_holder = lax.optimization_barrier((total, holder))
    outgoing = pack_queries(queries, valid, late_holder, groups)
    query_blocks = lax.all_to_all(outgoing, "dp", 0, 0, tiled=True)
    far, across_below, across_above, total, mix_last, to_last, outgoing = lax.optimization_barrier(
        (far, across_below, across_above, total, mix_last, to_last, outgoing)
    )

    far_keys, far_values = send(across_below[:1], Z_UP), send(across_above[1:], Z_DOWN)
    mix_next = across_x(to_last, -1)
    total = project(
        encoded,
        with_twin(2, 0, far) + with_twin(-1, 1, across_below) + with_twin(1, 1, across_above),
        total,
    )
    far_keys, far_values, total, mix_next, to_far, query_blocks = lax.optimization_barrier(
        (far_keys, far_values, total, mix_next, to_far, query_blocks)
    )

    mix_far = across_x(to_far, 2)
    parts = attend(encoded, with_twin(2, 1, far_keys, far_values), total, owner, query_blocks)
    returned = lax.all_to_all(parts, "dp", 0, 0, tiled=True)
    lead = (M - 1) // 16 * 16
    attended = combine(holder, returned, *queries.shape, lead)

    near = [attended, across_x(attended, 1), across_x(attended, -1), across_x(attended, 2)]
    mine = [mix_own, mix_last, mix_next, mix_far]
    other = [send(block, CORE_SWAP) for block in mine]
    theirs = mix(jnp.stack([1 - y_lo, core]), near, mine, other, BF)
    arrived = lax.ppermute(theirs, "tensor", tensor_pairs(0, 1))
    ours = mix(jnp.stack([y_lo, core]), near, mine, other, F32)
    mixed = (ours + arrived.astype(F32)).astype(BF)
    return jnp.concatenate([jnp.zeros((lead, mixed.shape[1]), BF), mixed], axis=0)


def solution(mesh):
    placed = (
        P("dp", None, None),
        P(None, "dp", "tensor"),
        P("dp", "tensor"),
        P("tensor", None),
        P("dp", None, None, None),
        P(),
    )
    return jax.shard_map(
        body, mesh=mesh, in_specs=placed, out_specs=P("dp", "tensor"), check_vma=False
    )
```

```python
import functools
import math

import jax
import jax.numpy as jnp
from jax import lax
from jax.experimental import pallas as pl
from jax.experimental.pallas import tpu as pltpu
from jax.sharding import PartitionSpec as P

HD = 128
M = 64
BF = jnp.bfloat16
F32 = jnp.float32
ATTEND_SLOTS = 4
VMEM_LIMIT = 48 * 1024 * 1024


def dp_pairs(dz, dy, dc):
    pairs = []
    for i in range(16):
        z, y, c = i // 4, (i // 2) % 2, i % 2
        pairs.append((i, ((z + dz) % 4) * 4 + ((y + dy) % 2) * 2 + (c + dc) % 2))
    return pairs


def tensor_pairs(dx, dy):
    pairs = []
    for i in range(8):
        x, y = i // 2, i % 2
        pairs.append((i, ((x + dx) % 4) * 2 + (y + dy) % 2))
    return pairs


Z_UP, Z_DOWN = dp_pairs(1, 0, 0), dp_pairs(-1, 0, 0)
Y_SWAP, CORE_SWAP = dp_pairs(0, 1, 0), dp_pairs(0, 0, 1)


def vmem_specs(count):
    return [pl.BlockSpec(memory_space=pltpu.VMEM)] * count


def add_terms(sizes, rows, weight_refs, total, out):
    weights = []
    at = 0
    for size in sizes:
        if size == 1:
            weights.append((weight_refs[at].at[0], weight_refs[at].at[1]))
        else:
            weights.append((weight_refs[at].at[0], weight_refs[at + 1].at[0]))
        at += size
    columns = out.shape[1] // 2
    for side in range(2):
        cols = slice(side * columns, (side + 1) * columns)
        value = None if total is None else total[:, cols]
        for row, weight in zip(rows, weights):
            term = jnp.dot(row[...], weight[side][...], preferred_element_type=F32)
            value = term if value is None else value + term
        out[:, cols] = value.astype(out.dtype)


def project_kernel(sizes, has_total, idx, *refs):
    del idx
    blocks = len(sizes)
    rows, weights = refs[:blocks], refs[blocks : blocks + sum(sizes)]
    add_terms(sizes, rows, weights, refs[-2] if has_total else None, refs[-1])


def project_operands(encoded, pieces, tile):
    arrays = [array for _, weight in pieces for array in weight]
    depth = arrays[0].shape[1]
    specs = [
        pl.BlockSpec((tile, depth), lambda m, i, j=j: (m, i[j])) for j in range(len(pieces))
    ] + [
        pl.BlockSpec(array.shape, lambda m, i: (0, 0, 0), pipeline_mode=pl.Buffered(1))
        for array in arrays
    ]
    return specs, [encoded] * len(pieces) + arrays


def project(encoded, pieces, total):
    rows = encoded.shape[0]
    depth, columns = pieces[0][1][0].shape[1:]
    tile = 256
    in_specs, operands = project_operands(encoded, pieces, tile)
    total_spec = pl.BlockSpec((tile, 2 * columns), lambda m, i: (m, 0))
    if total is not None:
        in_specs.append(total_spec)
        operands.append(total)
    return pl.pallas_call(
        functools.partial(project_kernel, [len(w) for _, w in pieces], total is not None),
        grid_spec=pltpu.PrefetchScalarGridSpec(
            num_scalar_prefetch=1, grid=(rows // tile,), in_specs=in_specs, out_specs=total_spec
        ),
        out_shape=jax.ShapeDtypeStruct((rows, 2 * columns), F32),
        compiler_params=pltpu.CompilerParams(vmem_limit_bytes=VMEM_LIMIT),
        cost_estimate=pl.CostEstimate(
            flops=4 * rows * depth * columns * len(pieces),
            bytes_accessed=2 * len(pieces) * depth * (rows + 2 * columns),
            transcendentals=0,
        ),
        name="project",
    )(jnp.stack([place for place, _ in pieces]).astype(jnp.int32), *operands)


def split_kernel(place, *refs):
    del place
    count = len(refs) // 2
    for source, target in zip(refs[:count], refs[count:]):
        target[...] = source[...]


def split_rows(core, places, weight):
    parts = len(places)
    half, width = weight.shape[0] // 2, weight.shape[1] // parts
    tile = half // 4
    return pl.pallas_call(
        split_kernel,
        grid_spec=pltpu.PrefetchScalarGridSpec(
            num_scalar_prefetch=1,
            grid=(4,),
            in_specs=[
                pl.BlockSpec((tile, width), lambda m, place, r=r: (place[parts] * 4 + m, place[r]))
                for r in range(parts)
            ],
            out_specs=[pl.BlockSpec((tile, width), lambda m, place: (m, 0))] * parts,
        ),
        out_shape=[jax.ShapeDtypeStruct((half, width), weight.dtype)] * parts,
        compiler_params=pltpu.CompilerParams(vmem_limit_bytes=VMEM_LIMIT),
        cost_estimate=pl.CostEstimate(
            flops=0, bytes_accessed=half * width // 8, transcendentals=0
        ),
        name="split_rows",
    )(jnp.stack(places + [core]), *[weight] * parts)


def pack_kernel(holder, query, valid, out):
    rows = query.shape[0]
    shifted = pltpu.roll(query[...].astype(F32), rows - (M - 1), 0).astype(BF)
    heads = query.shape[1] // HD
    for j in range(valid.shape[0]):
        u = j // 2
        for h in range(heads):
            out[holder[j], h * M : (h + 1) * M, :] = shifted[
                u * M : (u + 1) * M, h * HD : (h + 1) * HD
            ]
        out[holder[j], heads * M :, :] = jnp.tile(valid[j : j + 1, :], (16, 1)).astype(BF)


def pack_queries(query, valid, holder, groups):
    return pl.pallas_call(
        pack_kernel,
        in_specs=[pl.BlockSpec(memory_space=pltpu.SMEM)] + vmem_specs(2),
        out_specs=pl.BlockSpec(memory_space=pltpu.VMEM),
        out_shape=jax.ShapeDtypeStruct((groups, query.shape[1] // HD * M + 16, HD), BF),
        compiler_params=pltpu.CompilerParams(vmem_limit_bytes=VMEM_LIMIT),
        name="pack_queries",
    )(holder, query, valid)


def attend_kernel(sizes, idx, *refs):
    blocks = len(sizes)
    rows, weights = refs[:blocks], refs[blocks : blocks + sum(sizes)]
    total, query, out, keys_values = refs[-4:]
    add_terms(sizes, rows, weights, total, keys_values)
    heads = keys_values.shape[1] // (2 * HD)
    span = keys_values.shape[0] // ATTEND_SLOTS
    lane = lax.broadcasted_iota(jnp.int32, (M, HD), 1)
    pairs = [(i, h) for i in range(ATTEND_SLOTS) for h in range(heads)]
    places = [idx[blocks + pl.program_id(0) * ATTEND_SLOTS + i] for i in range(ATTEND_SLOTS)]
    scores = {}
    for i, h in pairs:
        cols = slice(h * HD, (h + 1) * HD)
        scores[i, h] = lax.dot_general(
            query[places[i], h * M : (h + 1) * M, :],
            keys_values[i * span : (i + 1) * span, cols],
            (((1,), (1,)), ((), ())),
            preferred_element_type=F32,
        )
    valid = [query[place, heads * M : heads * M + 1, :span].astype(F32) > 0.5 for place in places]
    shares, levels = {}, {}
    for i, h in pairs:
        scaled = jnp.where(valid[i], scores[i, h] * (1.0 / math.sqrt(HD)), -jnp.inf)
        highest = jnp.max(scaled, axis=1, keepdims=True)
        raised = jnp.exp(scaled - highest)
        norm = jnp.sum(raised, axis=1, keepdims=True)
        shares[i, h] = (raised / norm).astype(BF)
        levels[i, h] = highest + jnp.log(norm)
    for i, h in pairs:
        out[places[i], h * M : (h + 1) * M, :] = jnp.dot(
            shares[i, h],
            keys_values[i * span : (i + 1) * span, (heads + h) * HD : (heads + h + 1) * HD],
            preferred_element_type=F32,
        ).astype(BF)
    for i in range(ATTEND_SLOTS):
        stats = jnp.zeros((M, HD), F32)
        for h in range(heads):
            first = levels[i, h].astype(BF).astype(F32)
            second = (levels[i, h] - first).astype(BF).astype(F32)
            third = levels[i, h] - first - second
            stats = jnp.where(lane == h, first, stats)
            stats = jnp.where(lane == heads + h, second, stats)
            stats = jnp.where(lane == 2 * heads + h, third, stats)
        square = jnp.concatenate([stats, jnp.zeros((HD - M, HD), F32)], axis=0)
        out[places[i], heads * M :, :] = square.T[:16].astype(BF)


def attend(encoded, pieces, total, owner, query_blocks):
    rows = encoded.shape[0]
    tile = rows // owner.shape[0] * ATTEND_SLOTS
    in_specs, operands = project_operands(encoded, pieces, tile)
    places = jnp.concatenate([jnp.stack([place for place, _ in pieces]).astype(jnp.int32), owner])
    return pl.pallas_call(
        functools.partial(attend_kernel, [len(w) for _, w in pieces]),
        grid_spec=pltpu.PrefetchScalarGridSpec(
            num_scalar_prefetch=1,
            grid=(rows // tile,),
            in_specs=in_specs
            + [
                pl.BlockSpec((tile, total.shape[1]), lambda m, i: (m, 0)),
                pl.BlockSpec(query_blocks.shape, lambda m, i: (0, 0, 0)),
            ],
            out_specs=pl.BlockSpec(query_blocks.shape, lambda m, i: (0, 0, 0)),
            scratch_shapes=[pltpu.VMEM((tile, total.shape[1]), BF)],
        ),
        out_shape=jax.ShapeDtypeStruct(query_blocks.shape, BF),
        compiler_params=pltpu.CompilerParams(vmem_limit_bytes=VMEM_LIMIT),
        name="attend",
    )(places, *operands, total, query_blocks)


def combine_kernel(lead, holder, parts, out):
    rows, columns = out.shape[0] + lead, out.shape[1]
    heads, stretches = columns // HD, rows // M
    shares = []
    for u in range(stretches):
        levels = []
        for n in range(2):
            stats = parts[holder[2 * u + n], heads * M :, :].astype(F32)
            levels.append(stats[:heads] + stats[heads : 2 * heads] + stats[2 * heads : 3 * heads])
        top = jnp.maximum(levels[0], levels[1])
        raised = [jnp.exp(level - top) for level in levels]
        both = raised[0] + raised[1]
        shares += [raised[0] / both, raised[1] / both]
    used = 2 * stretches * heads
    share_columns = jnp.concatenate(shares + [jnp.zeros((HD - used, HD), F32)], axis=0).T
    flat = []
    for u in range(stretches):
        pieces = []
        for h in range(heads):
            terms = []
            for n in range(2):
                at = (2 * u + n) * heads + h
                part = parts[holder[2 * u + n], h * M : (h + 1) * M, :].astype(F32)
                terms.append(part * share_columns[:M, at : at + 1])
            pieces.append(terms[0] + terms[1])
        flat.append(jnp.concatenate(pieces, axis=1))
    shifted = pltpu.roll(jnp.concatenate(flat, axis=0), M - 1, 0)
    row = lax.broadcasted_iota(jnp.int32, (rows, columns), 0)
    out[...] = jnp.where(row >= M - 1, shifted, 0.0)[lead:].astype(BF)


def combine(holder, parts, rows, columns, lead):
    return pl.pallas_call(
        functools.partial(combine_kernel, lead),
        in_specs=[pl.BlockSpec(memory_space=pltpu.SMEM)] + vmem_specs(1),
        out_specs=pl.BlockSpec(memory_space=pltpu.VMEM),
        out_shape=jax.ShapeDtypeStruct((rows - lead, columns), BF),
        compiler_params=pltpu.CompilerParams(vmem_limit_bytes=VMEM_LIMIT),
        name="combine",
    )(holder, parts)


def mix_kernel(place, *refs):
    attended, mine, other, out = refs[:4], refs[4:8], refs[8:12], refs[12]
    core = place[1]
    half = mine[0].shape[0]
    total = None
    for r in range(4):
        for swap, weight in ((0, mine[r]), (1, other[r])):
            cols = pl.ds(pl.multiple_of(((core + swap) % 2) * half, half), half)
            term = jnp.dot(attended[r][:, cols], weight[...], preferred_element_type=F32)
            total = term if total is None else total + term
    out[...] = total.astype(out.dtype)


def mix(place, attended, mine, other, kind):
    rows, columns = attended[0].shape
    half, width = mine[0].shape[0], mine[0].shape[1] // 2
    tile = width // 2
    weight_spec = pl.BlockSpec((half, tile), lambda j, place: (0, place[0] * 2 + j))
    return pl.pallas_call(
        mix_kernel,
        grid_spec=pltpu.PrefetchScalarGridSpec(
            num_scalar_prefetch=1,
            grid=(2,),
            in_specs=[pl.BlockSpec((rows, columns), lambda j, place: (0, 0))] * 4
            + [weight_spec] * 8,
            out_specs=pl.BlockSpec((rows, tile), lambda j, place: (0, j)),
        ),
        out_shape=jax.ShapeDtypeStruct((rows, width), kind),
        compiler_params=pltpu.CompilerParams(vmem_limit_bytes=VMEM_LIMIT),
        cost_estimate=pl.CostEstimate(
            flops=8 * rows * columns * width, bytes_accessed=8 * columns * width, transcendentals=0
        ),
        name="mix",
    )(place, *attended, *mine, *other)


def body(encoded_neighbours, kv_weight, queries, out_weight, neighbour_ids, slot_map):
    groups = lax.axis_size("dp")
    position = lax.axis_index("dp")
    tensor_at = lax.axis_index("tensor")
    z, y, core = position // 4, (position // 2) % 2, position % 2
    x, y_lo = tensor_at // 2, tensor_at % 2
    slot_count, span, model_width = encoded_neighbours.shape
    encoded = encoded_neighbours.reshape(slot_count * span, model_width)
    held = lax.dynamic_slice_in_dim(slot_map, position * slot_count, slot_count)
    owner = held // slot_count
    wanted = position * slot_count + jnp.arange(slot_count, dtype=jnp.int32)
    holder = (
        jnp.sum(
            jnp.where(
                slot_map[None, :] == wanted[:, None],
                jnp.arange(slot_map.shape[0], dtype=jnp.int32)[None, :],
                0,
            ),
            axis=1,
        )
        // slot_count
    )
    valid = (neighbour_ids.reshape(slot_count, span) != 0).astype(F32)

    def send(block, pairs):
        return lax.ppermute(block, "dp", pairs)

    def across_x(block, step):
        return lax.ppermute(block, "tensor", tensor_pairs(step, 0))

    def with_twin(dz, dy, *arrays):
        def at(dc):
            return ((z + dz) % 4) * 4 + ((y + dy) % 2) * 2 + (core + dc) % 2

        return [(at(0), arrays), (at(1), tuple(send(array, CORE_SWAP) for array in arrays))]

    own = kv_weight
    below, above, across = send(own, Z_UP), send(own, Z_DOWN), send(own, Y_SWAP)
    mix_own, to_next, to_last, to_far = split_rows(
        core, [x, (x + 1) % 4, (x + 3) % 4, (x + 2) % 4], out_weight
    )
    total = project(encoded, with_twin(0, 0, own), None)
    below, above, total, to_next = lax.optimization_barrier((below, above, total, to_next))

    far, across_below, across_above = send(above, Z_DOWN), send(across, Z_UP), send(above, Y_SWAP)
    mix_last = across_x(to_next, 1)
    total = project(
        encoded,
        with_twin(-1, 0, below) + with_twin(1, 0, above) + with_twin(0, 1, across),
        total,
    )
    total, late_holder = lax.optimization_barrier((total, holder))
    outgoing = pack_queries(queries, valid, late_holder, groups)
    query_blocks = lax.all_to_all(outgoing, "dp", 0, 0, tiled=True)
    across_below, across_above, total, mix_last, to_last, outgoing = lax.optimization_barrier(
        (across_below, across_above, total, mix_last, to_last, outgoing)
    )

    far_keys, far_values = send(across_below[:1], Z_UP), send(across_above[1:], Z_DOWN)
    mix_next = across_x(to_last, -1)
    total = project(
        encoded,
        with_twin(2, 0, far) + with_twin(-1, 1, across_below) + with_twin(1, 1, across_above),
        total,
    )
    far_keys, far_values, total, mix_next, to_far, query_blocks = lax.optimization_barrier(
        (far_keys, far_values, total, mix_next, to_far, query_blocks)
    )

    mix_far = across_x(to_far, 2)
    parts = attend(encoded, with_twin(2, 1, far_keys, far_values), total, owner, query_blocks)
    returned = lax.all_to_all(parts, "dp", 0, 0, tiled=True)
    lead = (M - 1) // 16 * 16
    attended = combine(holder, returned, *queries.shape, lead)

    near = [attended, across_x(attended, 1), across_x(attended, -1), across_x(attended, 2)]
    mine = [mix_own, mix_last, mix_next, mix_far]
    other = [send(block, CORE_SWAP) for block in mine]
    theirs = mix(jnp.stack([1 - y_lo, core]), near, mine, other, BF)
    arrived = lax.ppermute(theirs, "tensor", tensor_pairs(0, 1))
    ours = mix(jnp.stack([y_lo, core]), near, mine, other, F32)
    mixed = (ours + arrived.astype(F32)).astype(BF)
    return jnp.concatenate([jnp.zeros((lead, mixed.shape[1]), BF), mixed], axis=0)


def solution(mesh):
    placed = (
        P("dp", None, None),
        P(None, "dp", "tensor"),
        P("dp", "tensor"),
        P("tensor", None),
        P("dp", None, None, None),
        P(),
    )
    return jax.shard_map(
        body, mesh=mesh, in_specs=placed, out_specs=P("dp", "tensor"), check_vma=False
    )
```

```python
import functools
import math

import jax
import jax.numpy as jnp
from jax import lax
from jax.experimental import pallas as pl
from jax.experimental.pallas import tpu as pltpu
from jax.sharding import PartitionSpec as P

HD = 128
M = 64
BF = jnp.bfloat16
F32 = jnp.float32
ATTEND_SLOTS = 4
VMEM_LIMIT = 48 * 1024 * 1024


def dp_pairs(dz, dy, dc):
    pairs = []
    for i in range(16):
        z, y, c = i // 4, (i // 2) % 2, i % 2
        pairs.append((i, ((z + dz) % 4) * 4 + ((y + dy) % 2) * 2 + (c + dc) % 2))
    return pairs


def tensor_pairs(dx, dy):
    pairs = []
    for i in range(8):
        x, y = i // 2, i % 2
        pairs.append((i, ((x + dx) % 4) * 2 + (y + dy) % 2))
    return pairs


Z_UP, Z_DOWN = dp_pairs(1, 0, 0), dp_pairs(-1, 0, 0)
Y_SWAP, CORE_SWAP = dp_pairs(0, 1, 0), dp_pairs(0, 0, 1)


def vmem_specs(count):
    return [pl.BlockSpec(memory_space=pltpu.VMEM)] * count


def add_terms(sizes, rows, weight_refs, total, out):
    weights = []
    at = 0
    for size in sizes:
        if size == 1:
            weights.append((weight_refs[at].at[0], weight_refs[at].at[1]))
        else:
            weights.append((weight_refs[at].at[0], weight_refs[at + 1].at[0]))
        at += size
    columns = out.shape[1] // 2
    for side in range(2):
        cols = slice(side * columns, (side + 1) * columns)
        value = None if total is None else total[:, cols]
        for row, weight in zip(rows, weights):
            term = jnp.dot(row[...], weight[side][...], preferred_element_type=F32)
            value = term if value is None else value + term
        out[:, cols] = value.astype(out.dtype)


def project_kernel(sizes, has_total, idx, *refs):
    del idx
    blocks = len(sizes)
    rows, weights = refs[:blocks], refs[blocks : blocks + sum(sizes)]
    add_terms(sizes, rows, weights, refs[-2] if has_total else None, refs[-1])


def project_operands(encoded, pieces, tile):
    arrays = [array for _, weight in pieces for array in weight]
    depth = arrays[0].shape[1]
    specs = [
        pl.BlockSpec((tile, depth), lambda m, i, j=j: (m, i[j])) for j in range(len(pieces))
    ] + [
        pl.BlockSpec(array.shape, lambda m, i: (0, 0, 0), pipeline_mode=pl.Buffered(1))
        for array in arrays
    ]
    return specs, [encoded] * len(pieces) + arrays


def project(encoded, pieces, total):
    rows = encoded.shape[0]
    depth, columns = pieces[0][1][0].shape[1:]
    tile = 256
    in_specs, operands = project_operands(encoded, pieces, tile)
    total_spec = pl.BlockSpec((tile, 2 * columns), lambda m, i: (m, 0))
    if total is not None:
        in_specs.append(total_spec)
        operands.append(total)
    return pl.pallas_call(
        functools.partial(project_kernel, [len(w) for _, w in pieces], total is not None),
        grid_spec=pltpu.PrefetchScalarGridSpec(
            num_scalar_prefetch=1, grid=(rows // tile,), in_specs=in_specs, out_specs=total_spec
        ),
        out_shape=jax.ShapeDtypeStruct((rows, 2 * columns), F32),
        compiler_params=pltpu.CompilerParams(vmem_limit_bytes=VMEM_LIMIT),
        cost_estimate=pl.CostEstimate(
            flops=4 * rows * depth * columns * len(pieces),
            bytes_accessed=2 * len(pieces) * depth * (rows + 2 * columns),
            transcendentals=0,
        ),
        name="project",
    )(jnp.stack([place for place, _ in pieces]).astype(jnp.int32), *operands)


def split_kernel(place, *refs):
    del place
    count = len(refs) // 2
    for source, target in zip(refs[:count], refs[count:]):
        target[...] = source[...]


def split_rows(core, places, weight):
    parts = len(places)
    half, width = weight.shape[0] // 2, weight.shape[1] // parts
    tile = half // 4
    return pl.pallas_call(
        split_kernel,
        grid_spec=pltpu.PrefetchScalarGridSpec(
            num_scalar_prefetch=1,
            grid=(4,),
            in_specs=[
                pl.BlockSpec((tile, width), lambda m, place, r=r: (place[parts] * 4 + m, place[r]))
                for r in range(parts)
            ],
            out_specs=[pl.BlockSpec((tile, width), lambda m, place: (m, 0))] * parts,
        ),
        out_shape=[jax.ShapeDtypeStruct((half, width), weight.dtype)] * parts,
        compiler_params=pltpu.CompilerParams(vmem_limit_bytes=VMEM_LIMIT),
        cost_estimate=pl.CostEstimate(
            flops=0, bytes_accessed=half * width // 8, transcendentals=0
        ),
        name="split_rows",
    )(jnp.stack(places + [core]), *[weight] * parts)


def pack_kernel(holder, query, valid, out):
    rows = query.shape[0]
    shifted = pltpu.roll(query[...].astype(F32), rows - (M - 1), 0).astype(BF)
    heads = query.shape[1] // HD
    for j in range(valid.shape[0]):
        u = j // 2
        for h in range(heads):
            out[holder[j], h * M : (h + 1) * M, :] = shifted[
                u * M : (u + 1) * M, h * HD : (h + 1) * HD
            ]
        out[holder[j], heads * M :, :] = jnp.tile(valid[j : j + 1, :], (16, 1)).astype(BF)


def pack_queries(query, valid, holder, groups):
    return pl.pallas_call(
        pack_kernel,
        in_specs=[pl.BlockSpec(memory_space=pltpu.SMEM)] + vmem_specs(2),
        out_specs=pl.BlockSpec(memory_space=pltpu.VMEM),
        out_shape=jax.ShapeDtypeStruct((groups, query.shape[1] // HD * M + 16, HD), BF),
        compiler_params=pltpu.CompilerParams(vmem_limit_bytes=VMEM_LIMIT),
        name="pack_queries",
    )(holder, query, valid)


def attend_kernel(sizes, idx, *refs):
    blocks = len(sizes)
    rows, weights = refs[:blocks], refs[blocks : blocks + sum(sizes)]
    total, query, out, keys_values = refs[-4:]
    add_terms(sizes, rows, weights, total, keys_values)
    heads = keys_values.shape[1] // (2 * HD)
    span = keys_values.shape[0] // ATTEND_SLOTS
    lane = lax.broadcasted_iota(jnp.int32, (M, HD), 1)
    pairs = [(i, h) for i in range(ATTEND_SLOTS) for h in range(heads)]
    places = [idx[blocks + pl.program_id(0) * ATTEND_SLOTS + i] for i in range(ATTEND_SLOTS)]
    scores = {}
    for i, h in pairs:
        cols = slice(h * HD, (h + 1) * HD)
        scores[i, h] = lax.dot_general(
            query[places[i], h * M : (h + 1) * M, :],
            keys_values[i * span : (i + 1) * span, cols],
            (((1,), (1,)), ((), ())),
            preferred_element_type=F32,
        )
    valid = [query[place, heads * M : heads * M + 1, :span].astype(F32) > 0.5 for place in places]
    shares, levels = {}, {}
    for i, h in pairs:
        scaled = jnp.where(valid[i], scores[i, h] * (1.0 / math.sqrt(HD)), -jnp.inf)
        highest = jnp.max(scaled, axis=1, keepdims=True)
        raised = jnp.exp(scaled - highest)
        norm = jnp.sum(raised, axis=1, keepdims=True)
        shares[i, h] = (raised / norm).astype(BF)
        levels[i, h] = highest + jnp.log(norm)
    for i, h in pairs:
        out[places[i], h * M : (h + 1) * M, :] = jnp.dot(
            shares[i, h],
            keys_values[i * span : (i + 1) * span, (heads + h) * HD : (heads + h + 1) * HD],
            preferred_element_type=F32,
        ).astype(BF)
    for i in range(ATTEND_SLOTS):
        stats = jnp.zeros((M, HD), F32)
        for h in range(heads):
            first = levels[i, h].astype(BF).astype(F32)
            second = (levels[i, h] - first).astype(BF).astype(F32)
            third = levels[i, h] - first - second
            stats = jnp.where(lane == h, first, stats)
            stats = jnp.where(lane == heads + h, second, stats)
            stats = jnp.where(lane == 2 * heads + h, third, stats)
        square = jnp.concatenate([stats, jnp.zeros((HD - M, HD), F32)], axis=0)
        out[places[i], heads * M :, :] = square.T[:16].astype(BF)


def attend(encoded, pieces, total, owner, query_blocks):
    rows = encoded.shape[0]
    tile = rows // owner.shape[0] * ATTEND_SLOTS
    in_specs, operands = project_operands(encoded, pieces, tile)
    places = jnp.concatenate([jnp.stack([place for place, _ in pieces]).astype(jnp.int32), owner])
    return pl.pallas_call(
        functools.partial(attend_kernel, [len(w) for _, w in pieces]),
        grid_spec=pltpu.PrefetchScalarGridSpec(
            num_scalar_prefetch=1,
            grid=(rows // tile,),
            in_specs=in_specs
            + [
                pl.BlockSpec((tile, total.shape[1]), lambda m, i: (m, 0)),
                pl.BlockSpec(query_blocks.shape, lambda m, i: (0, 0, 0)),
            ],
            out_specs=pl.BlockSpec(query_blocks.shape, lambda m, i: (0, 0, 0)),
            scratch_shapes=[pltpu.VMEM((tile, total.shape[1]), BF)],
        ),
        out_shape=jax.ShapeDtypeStruct(query_blocks.shape, BF),
        compiler_params=pltpu.CompilerParams(vmem_limit_bytes=VMEM_LIMIT),
        name="attend",
    )(places, *operands, total, query_blocks)


def combine_kernel(lead, holder, parts, out):
    rows, columns = out.shape[0] + lead, out.shape[1]
    heads, stretches = columns // HD, rows // M
    shares = []
    for u in range(stretches):
        levels = []
        for n in range(2):
            stats = parts[holder[2 * u + n], heads * M :, :].astype(F32)
            levels.append(stats[:heads] + stats[heads : 2 * heads] + stats[2 * heads : 3 * heads])
        top = jnp.maximum(levels[0], levels[1])
        raised = [jnp.exp(level - top) for level in levels]
        both = raised[0] + raised[1]
        shares += [raised[0] / both, raised[1] / both]
    used = 2 * stretches * heads
    share_columns = jnp.concatenate(shares + [jnp.zeros((HD - used, HD), F32)], axis=0).T
    flat = []
    for u in range(stretches):
        pieces = []
        for h in range(heads):
            terms = []
            for n in range(2):
                at = (2 * u + n) * heads + h
                part = parts[holder[2 * u + n], h * M : (h + 1) * M, :].astype(F32)
                terms.append(part * share_columns[:M, at : at + 1])
            pieces.append(terms[0] + terms[1])
        flat.append(jnp.concatenate(pieces, axis=1))
    shifted = pltpu.roll(jnp.concatenate(flat, axis=0), M - 1, 0)
    row = lax.broadcasted_iota(jnp.int32, (rows, columns), 0)
    out[...] = jnp.where(row >= M - 1, shifted, 0.0)[lead:].astype(BF)


def combine(holder, parts, rows, columns, lead):
    return pl.pallas_call(
        functools.partial(combine_kernel, lead),
        in_specs=[pl.BlockSpec(memory_space=pltpu.SMEM)] + vmem_specs(1),
        out_specs=pl.BlockSpec(memory_space=pltpu.VMEM),
        out_shape=jax.ShapeDtypeStruct((rows - lead, columns), BF),
        compiler_params=pltpu.CompilerParams(vmem_limit_bytes=VMEM_LIMIT),
        name="combine",
    )(holder, parts)


def mix_kernel(place, *refs):
    attended, mine, other, out = refs[:4], refs[4:8], refs[8:12], refs[12]
    core = place[1]
    half = mine[0].shape[0]
    total = None
    for r in range(4):
        for swap, weight in ((0, mine[r]), (1, other[r])):
            cols = pl.ds(pl.multiple_of(((core + swap) % 2) * half, half), half)
            term = jnp.dot(attended[r][:, cols], weight[...], preferred_element_type=F32)
            total = term if total is None else total + term
    out[...] = total.astype(out.dtype)


def mix(place, attended, mine, other, kind):
    rows, columns = attended[0].shape
    half, width = mine[0].shape[0], mine[0].shape[1] // 2
    tile = width // 2
    weight_spec = pl.BlockSpec((half, tile), lambda j, place: (0, place[0] * 2 + j))
    return pl.pallas_call(
        mix_kernel,
        grid_spec=pltpu.PrefetchScalarGridSpec(
            num_scalar_prefetch=1,
            grid=(2,),
            in_specs=[pl.BlockSpec((rows, columns), lambda j, place: (0, 0))] * 4
            + [weight_spec] * 8,
            out_specs=pl.BlockSpec((rows, tile), lambda j, place: (0, j)),
        ),
        out_shape=jax.ShapeDtypeStruct((rows, width), kind),
        compiler_params=pltpu.CompilerParams(vmem_limit_bytes=VMEM_LIMIT),
        cost_estimate=pl.CostEstimate(
            flops=8 * rows * columns * width, bytes_accessed=8 * columns * width, transcendentals=0
        ),
        name="mix",
    )(place, *attended, *mine, *other)


def body(encoded_neighbours, kv_weight, queries, out_weight, neighbour_ids, slot_map):
    groups = lax.axis_size("dp")
    position = lax.axis_index("dp")
    tensor_at = lax.axis_index("tensor")
    z, y, core = position // 4, (position // 2) % 2, position % 2
    x, y_lo = tensor_at // 2, tensor_at % 2
    slot_count, span, model_width = encoded_neighbours.shape
    encoded = encoded_neighbours.reshape(slot_count * span, model_width)
    held = lax.dynamic_slice_in_dim(slot_map, position * slot_count, slot_count)
    owner = held // slot_count
    wanted = position * slot_count + jnp.arange(slot_count, dtype=jnp.int32)
    holder = (
        jnp.sum(
            jnp.where(
                slot_map[None, :] == wanted[:, None],
                jnp.arange(slot_map.shape[0], dtype=jnp.int32)[None, :],
                0,
            ),
            axis=1,
        )
        // slot_count
    )
    valid = (neighbour_ids.reshape(slot_count, span) != 0).astype(F32)

    def send(block, pairs):
        return lax.ppermute(block, "dp", pairs)

    def across_x(block, step):
        return lax.ppermute(block, "tensor", tensor_pairs(step, 0))

    def with_twin(dz, dy, *arrays):
        def at(dc):
            return ((z + dz) % 4) * 4 + ((y + dy) % 2) * 2 + (core + dc) % 2

        return [(at(0), arrays), (at(1), tuple(send(array, CORE_SWAP) for array in arrays))]

    own = kv_weight
    below, above, across = send(own, Z_UP), send(own, Z_DOWN), send(own, Y_SWAP)
    mix_own, to_next, to_last, to_far = split_rows(
        core, [x, (x + 1) % 4, (x + 3) % 4, (x + 2) % 4], out_weight
    )
    total = project(encoded, with_twin(0, 0, own), None)
    below, above, total, to_next, to_last = lax.optimization_barrier(
        (below, above, total, to_next, to_last)
    )

    far, across_below, across_above = send(above, Z_DOWN), send(across, Z_UP), send(above, Y_SWAP)
    mix_last, mix_next = across_x(to_next, 1), across_x(to_last, -1)
    total = project(
        encoded,
        with_twin(-1, 0, below) + with_twin(1, 0, above) + with_twin(0, 1, across),
        total,
    )
    total, late_holder = lax.optimization_barrier((total, holder))
    outgoing = pack_queries(queries, valid, late_holder, groups)
    query_blocks = lax.all_to_all(outgoing, "dp", 0, 0, tiled=True)
    across_below, across_above, total, mix_last, mix_next, to_far, outgoing = (
        lax.optimization_barrier(
            (across_below, across_above, total, mix_last, mix_next, to_far, outgoing)
        )
    )

    far_keys, far_values = send(across_below[:1], Z_UP), send(across_above[1:], Z_DOWN)
    mix_far = across_x(to_far, 2)
    total = project(
        encoded,
        with_twin(2, 0, far) + with_twin(-1, 1, across_below) + with_twin(1, 1, across_above),
        total,
    )
    far_keys, far_values, total, mix_far, query_blocks = lax.optimization_barrier(
        (far_keys, far_values, total, mix_far, query_blocks)
    )

    parts = attend(encoded, with_twin(2, 1, far_keys, far_values), total, owner, query_blocks)
    returned = lax.all_to_all(parts, "dp", 0, 0, tiled=True)
    lead = (M - 1) // 16 * 16
    attended = combine(holder, returned, *queries.shape, lead)

    near = [attended, across_x(attended, 1), across_x(attended, -1), across_x(attended, 2)]
    mine = [mix_own, mix_last, mix_next, mix_far]
    other = [send(block, CORE_SWAP) for block in mine]
    theirs = mix(jnp.stack([1 - y_lo, core]), near, mine, other, BF)
    arrived = lax.ppermute(theirs, "tensor", tensor_pairs(0, 1))
    ours = mix(jnp.stack([y_lo, core]), near, mine, other, F32)
    mixed = (ours + arrived.astype(F32)).astype(BF)
    return jnp.concatenate([jnp.zeros((lead, mixed.shape[1]), BF), mixed], axis=0)


def solution(mesh):
    placed = (
        P("dp", None, None),
        P(None, "dp", "tensor"),
        P("dp", "tensor"),
        P("tensor", None),
        P("dp", None, None, None),
        P(),
    )
    return jax.shard_map(
        body, mesh=mesh, in_specs=placed, out_specs=P("dp", "tensor"), check_vma=False
    )
```
